512 devices in a mesh: dp: 4 (over x), expert: 128 (over z, y, core).
Axes of the slice: x: 4, y: 4, z: 16, core: 2. Of those that a mesh axis runs over, the one named last changes fastest.
Arguments:
- tokens: bfloat16 [65536, 2048], P(('dp', 'expert')), may hold values from -6 to 6
- cotangent: bfloat16 [65536, 2048], P(('dp', 'expert')), may hold values from -0.59765625 to 0.59765625
- gate_values: bfloat16 [65536, 4], P(('dp', 'expert')), may hold values from 0.049804688 to 0.59765625
- expert_ids: int32 [65536, 4], P(('dp', 'expert')), may hold values from 0 to 127, all different within a row
- hot_plan: int32 [128], replicated, may hold values from 0 to 1, as said below
- expert_caps: int32 [128], replicated, may hold values from 1 to 4
- w_up: bfloat16 [128, 2048, 384], P('expert'), may hold values from -0.125 to 0.125
- w_down: bfloat16 [128, 384, 2048], P('expert'), may hold values from -0.3125 to 0.3125
Outputs:
- grad_up: bfloat16 [128, 2048, 384], P('expert', 'dp')
- grad_down: bfloat16 [128, 384, 2048], P('expert', None, 'dp')
- gate_grad: float32 [65536, 4], P(('dp', 'expert'))
The draws below stay inside these ranges and needn't reach their ends.
Inputs may be any that keep to these rules, and one draw needn't show every extreme that they name: hot_plan holds 0 or 1; the entries of experts 0 and 126 are always 1.
All inputs are finite; a program needn't handle non-finite values.
Results may differ from the reference program's by a relative error of at most 0.013.
Values may be sent and summed in bfloat16 or wider, within the bound.
No kernel may reach another device: no remote copies, remote signals or barrier semaphores. Data moves between devices by JAX's collectives and lax.ppermute only.
A program may use at most 64 MiB of HBM per device.

```python
import jax
import jax.numpy as jnp
from jax import lax

D = 2048
FW = 384
TOPK = 4
TOK_DEV = 128
EXPERTS = 128
CAP = 4
TOKENS = 65536
N_DP = 4


def draw_hot_plan(key, part):
    key = jax.random.fold_in(key, 7)
    picked = jax.random.randint(key, (EXPERTS,), 0, 4, dtype=jnp.int32) == 0
    places = jnp.arange(EXPERTS, dtype=jnp.int32)
    forced = (places == EXPERTS - 2) | (places == 0)
    return (picked | forced).astype(jnp.int32)


def place_ends(values, own_key, least, top_value):
    extent = values.shape
    spot = [jax.random.randint(jax.random.fold_in(own_key, axis), (), 0, extent[axis]) for axis in range(len(extent))]
    values = values.at[tuple(spot)].set(least)
    longest = extent.index(max(extent))
    spot[longest] = (spot[longest] + 1) % extent[longest]
    return values.at[tuple(spot)].set(top_value)


def levels(rng, dims, pieces, low, largest):
    gain = 1.0
    for axis_at, blocks in pieces:
        draws = jax.random.uniform(jax.random.fold_in(jax.random.fold_in(rng, 6), axis_at), (blocks,), jnp.float32, low / len(pieces), largest / len(pieces))
        gain = gain * jnp.repeat(jnp.exp(draws), dims[axis_at] // blocks).reshape((-1,) + (1,) * (len(dims) - 1 - axis_at))
    return gain


def distinct(own_key, rows, count, top, lift):
    ranking = jax.random.permutation(jax.random.fold_in(own_key, 1), count)
    pull = ranking
    for power in range(3):
        pull = pull * pull // count
    pull = pull * lift // count
    chance = jax.random.randint(jax.random.fold_in(own_key, 2), (rows, count), 0, 4096) + pull
    sure = jax.random.permutation(jax.random.fold_in(own_key, 3), rows)[jnp.arange(count) % rows]
    chance = jnp.where(jnp.arange(rows)[:, None] == sure[None, :], 1 << 14, chance)
    priority = chance * count + jnp.arange(count)
    return lax.top_k(priority.astype(jnp.int32), top)[1].astype(jnp.int32)


def gaussian(stream_key, dims, spread, bound, cuts=(), held_as=jnp.bfloat16):
    array = spread * jax.random.normal(stream_key, dims, jnp.float32)
    if cuts:
        array = array * levels(stream_key, dims, cuts, -0.22, 0.18)
    return jnp.clip(array, -bound, bound).astype(held_as)


def setup_inputs(seed: int = 0) -> dict:
    splits = jax.random.split(jax.random.key(seed), 9)
    return {
        "tokens": gaussian(splits[0], (TOKENS, D), 1.0, 6.0, ((0, 512),)),
        "cotangent": gaussian(splits[1], (TOKENS, D), 0.09, 0.59765625, ((0, 512),)),
        "gate_values": jnp.clip(0.049804688 + 0.54785156 * jax.random.uniform(splits[2], (TOKENS, TOPK), jnp.float32) ** levels(splits[2], (TOKENS, TOPK), ((0, 512),), -0.2, 0.2), 0.049804688, 0.59765625).astype(jnp.bfloat16),
        "expert_ids": distinct(splits[3], TOKENS, EXPERTS, TOPK, 512),
        "hot_plan": draw_hot_plan(jax.random.fold_in(splits[8], 71), 0),
        "expert_caps": place_ends(jax.random.randint(splits[5], (EXPERTS,), 1, CAP + 1), jax.random.fold_in(splits[5], 1), 1, CAP).astype(jnp.int32),
        "w_up": gaussian(splits[6], (EXPERTS, D, FW), D ** -0.5, 0.125, ((0, 128),)),
        "w_down": gaussian(splits[7], (EXPERTS, FW, D), FW ** -0.5, 0.3125, ((0, 128),)),
    }


def route_plan(id_flat, source, hot_plan, expert_caps, expert_count, capacity):
    expert_iota = jnp.arange(expert_count, dtype=jnp.int32)
    one_hot = (id_flat[:, None] == expert_iota[None, :]).astype(jnp.int32)
    earlier = jnp.cumsum(one_hot, axis=0) - one_hot
    expert_rank = jnp.sum(earlier * one_hot, axis=1)
    cap_of = jnp.sum(one_hot * expert_caps[None, :], axis=1)
    hot_of = jnp.sum(one_hot * hot_plan[None, :], axis=1)
    admitted = expert_rank < cap_of
    moved = (hot_of == 1) & (source % 2 == 1)
    target = jnp.where(moved, (id_flat + 1) % expert_count, id_flat).astype(jnp.int32)
    target_hot = (target[:, None] == expert_iota[None, :]).astype(jnp.int32)
    counted = target_hot * admitted[:, None].astype(jnp.int32)
    before = jnp.cumsum(counted, axis=0) - counted
    slot_rank = jnp.sum(before * target_hot, axis=1)
    kept_mask = admitted & (slot_rank < capacity)
    replica = target != id_flat
    return target, slot_rank, kept_mask, replica


def pack_slots(tokens, cotangent, gate_values, target, slot_rank, kept_mask, replica, expert_count, capacity):
    count = target.shape[0]
    width_d = tokens.shape[1]
    top_count = gate_values.shape[1]
    total = expert_count * capacity
    slot = jnp.where(kept_mask, target * capacity + slot_rank, total).astype(jnp.int32)
    filler = jnp.full((total + 1,), count, jnp.int32).at[slot].set(jnp.arange(count, dtype=jnp.int32))[:total]
    token_row = filler // top_count
    padded_x = jnp.concatenate([tokens, jnp.zeros((1, width_d), tokens.dtype)], axis=0)
    padded_dy = jnp.concatenate([cotangent, jnp.zeros((1, width_d), cotangent.dtype)], axis=0)
    sent_x = padded_x[token_row].reshape(expert_count, capacity, width_d)
    sent_dy = padded_dy[token_row].reshape(expert_count, capacity, width_d)
    gate_flat = jnp.concatenate([gate_values.reshape(-1), jnp.zeros((1,), gate_values.dtype)])[filler]
    rep_flat = jnp.concatenate([replica, jnp.zeros((1,), bool)])[filler]
    nothing = jnp.zeros_like(gate_flat)
    sent_gate = jnp.stack([jnp.where(rep_flat, nothing, gate_flat), jnp.where(rep_flat, gate_flat, nothing)], axis=-1)
    return sent_x, sent_dy, sent_gate.reshape(expert_count, capacity, 2), slot


def expert_pass(rows, dy_rows, gate_col, up_w, down_w):
    preact = jnp.dot(rows, up_w, preferred_element_type=jnp.float32)
    sigma = jax.nn.sigmoid(preact)
    hidden = (preact * sigma).astype(jnp.bfloat16)
    expert_out = jnp.dot(hidden, down_w, preferred_element_type=jnp.float32)
    gate_dot = jnp.sum(dy_rows.astype(jnp.float32) * expert_out, axis=1)
    scaled = (gate_col.astype(jnp.float32)[:, None] * dy_rows.astype(jnp.float32)).astype(jnp.bfloat16)
    grad_down = lax.dot_general(hidden, scaled, (((0,), (0,)), ((), ())), preferred_element_type=jnp.float32)
    backprop = lax.dot_general(scaled, down_w, (((1,), (1,)), ((), ())), preferred_element_type=jnp.float32)
    grad_pre = (backprop * sigma * (1.0 + preact * (1.0 - sigma))).astype(jnp.bfloat16)
    grad_up = lax.dot_general(rows, grad_pre, (((0,), (0,)), ((), ())), preferred_element_type=jnp.float32)
    return gate_dot, grad_up, grad_down


def reference(tokens, cotangent, gate_values, expert_ids, hot_plan, expert_caps, w_up, w_down):
    count = EXPERTS
    sum_up = jnp.zeros((count, D, FW), jnp.float32)
    sum_down = jnp.zeros((count, FW, D), jnp.float32)
    gate_blocks = []
    for group in range(N_DP):
        first_row = group * count * TOK_DEV
        last_row = first_row + count * TOK_DEV
        group_x = tokens[first_row:last_row].reshape(count, TOK_DEV, D)
        group_dy = cotangent[first_row:last_row].reshape(count, TOK_DEV, D)
        group_gate = gate_values[first_row:last_row].reshape(count, TOK_DEV, TOPK)
        group_ids = expert_ids[first_row:last_row].reshape(count, TOK_DEV * TOPK)

        def pack_source(source_item):
            x_block, dy_block, gate_block, id_block, source = source_item
            target, slot_rank, kept_mask, replica = route_plan(id_block, source, hot_plan, expert_caps, count, CAP)
            return pack_slots(x_block, dy_block, gate_block, target, slot_rank, kept_mask, replica, count, CAP)

        sent_x, sent_dy, sent_gate, slots = lax.map(
            pack_source, (group_x, group_dy, group_gate, group_ids, jnp.arange(count, dtype=jnp.int32)))

        def per_expert(expert):
            home_x = sent_x[:, expert].reshape(-1, D)
            home_dy = sent_dy[:, expert].reshape(-1, D)
            home_gate = sent_gate[:, expert, :, 0].reshape(-1)
            own_dot, own_up, own_down = expert_pass(home_x, home_dy, home_gate, w_up[expert], w_down[expert])
            helper = (expert + 1) % count
            help_x = sent_x[1::2, helper].reshape(-1, D)
            help_dy = sent_dy[1::2, helper].reshape(-1, D)
            help_gate = sent_gate[1::2, helper, :, 1].reshape(-1)
            rep_dot, rep_up, rep_down = expert_pass(help_x, help_dy, help_gate, w_up[expert], w_down[expert])
            rep_up_half = lax.optimization_barrier(rep_up.astype(jnp.bfloat16))
            rep_down_half = lax.optimization_barrier(rep_down.astype(jnp.bfloat16))
            part_up = (own_up + rep_up_half.astype(jnp.float32)).astype(jnp.bfloat16)
            part_down = (own_down + rep_down_half.astype(jnp.float32)).astype(jnp.bfloat16)
            own_value = jnp.where(home_gate > 0, own_dot, 0.0)
            rep_value = jnp.where(help_gate > 0, rep_dot, 0.0)
            return part_up, part_down, own_value, rep_value

        parts_up, parts_down, own_values, rep_values = lax.map(per_expert, jnp.arange(count, dtype=jnp.int32))
        sum_up = sum_up + parts_up.astype(jnp.float32)
        sum_down = sum_down + parts_down.astype(jnp.float32)
        rep_at = jnp.roll(rep_values, 1, axis=0).reshape(count, count // 2, 1, CAP)
        rep_full = jnp.concatenate([jnp.zeros_like(rep_at), rep_at], axis=2).reshape(count, count * CAP)
        slot_value = (own_values + rep_full).reshape(count, count, CAP)
        by_source = jnp.swapaxes(slot_value, 0, 1).reshape(count, count * CAP)
        padded = jnp.concatenate([by_source, jnp.zeros((count, 1), by_source.dtype)], axis=1)
        gate_block = jnp.take_along_axis(padded, slots, axis=1)
        gate_blocks.append(gate_block.reshape(count * TOK_DEV, TOPK))
    return sum_up.astype(jnp.bfloat16), sum_down.astype(jnp.bfloat16), jnp.concatenate(gate_blocks, axis=0)
```

```python
import functools

import jax
import jax.numpy as jnp
from jax import lax
from jax.experimental import pallas as pl
from jax.experimental.pallas import tpu as pltpu
from jax.sharding import PartitionSpec as P

SLOTS = 4
CHUNK = 2 * SLOTS


def contract(a, b, dims):
    return lax.dot_general(a, b, (dims, ((), ())), preferred_element_type=jnp.float32)


def route_pack(odd_ref, ids_ref, gates_ref, hot_ref, caps_ref, x_ref, dy_ref, sent_ref, code_ref):
    count = ids_ref.shape[0]
    experts = hot_ref.shape[1]
    wide = experts * CHUNK
    lane = lax.broadcasted_iota(jnp.int32, (count, experts), 1)
    row = lax.broadcasted_iota(jnp.int32, (count, count), 0)
    col = lax.broadcasted_iota(jnp.int32, (count, count), 1)
    below = (col < row).astype(jnp.bfloat16)
    picked = jnp.zeros((count, experts), jnp.float32)
    place = jnp.zeros((count, experts), jnp.float32)
    gate = jnp.zeros((count, experts), jnp.float32)
    for k in range(ids_ref.shape[1]):
        hit = ids_ref[:, k : k + 1] == lane
        picked = jnp.where(hit, 1.0, picked)
        place = jnp.where(hit, float(k), place)
        gate = jnp.where(hit, gates_ref[:, k : k + 1].astype(jnp.float32), gate)
    rank = contract(below, picked.astype(jnp.bfloat16), ((1,), (0,)))
    admitted = jnp.where(rank < caps_ref[...].astype(jnp.float32), picked, 0.0)
    moves = hot_ref[...].astype(jnp.float32) * odd_ref[0].astype(jnp.float32)
    moved = admitted * moves
    stay = admitted - moved
    moved_next = pltpu.roll(moved, 1, 1)
    stay_next = pltpu.roll(stay, experts - 1, 1)
    before = contract(below, (stay + moved_next).astype(jnp.bfloat16), ((1,), (0,)))
    tie_stay = jnp.where(pltpu.roll(place, 1, 1) < place, moved_next, 0.0)
    tie_move = jnp.where(pltpu.roll(place, experts - 1, 1) < place, stay_next, 0.0)
    slot = jnp.where(moves > 0, pltpu.roll(before, experts - 1, 1) + tie_move, before + tie_stay)
    code = jnp.where((admitted > 0) & (slot < SLOTS), rank, -8.0)
    code_ref[...] = code
    spread = (
        lax.broadcasted_iota(jnp.int32, (experts, wide), 1) // CHUNK
        == lax.broadcasted_iota(jnp.int32, (experts, wide), 0)
    ).astype(jnp.bfloat16)
    part = lax.broadcasted_iota(jnp.int32, (count, wide), 1) % CHUNK
    code_wide = contract(code.astype(jnp.bfloat16), spread, ((1,), (0,)))
    gate_wide = contract(gate.astype(jnp.bfloat16), spread, ((1,), (0,)))
    take_x = (code_wide == part.astype(jnp.float32)).astype(jnp.bfloat16)
    chosen = code_wide == (part - SLOTS).astype(jnp.float32)
    take_dy = chosen.astype(jnp.bfloat16)
    gate_pick = jnp.where(chosen, gate_wide, 0.0).astype(jnp.bfloat16)
    ones = jnp.ones((count, 128), jnp.bfloat16)
    gate_col = contract(gate_pick, ones, ((0,), (0,)))
    gate_col = jnp.concatenate([gate_col] * 4, axis=1)
    step = gate_col.shape[1]
    for c in range(x_ref.shape[1] // step):
        at = slice(c * step, (c + 1) * step)
        rows_x = contract(take_x, x_ref[:, at], ((0,), (0,)))
        rows_dy = contract(take_dy, dy_ref[:, at], ((0,), (0,)))
        sent_ref[:, at] = (rows_x + gate_col * rows_dy).astype(jnp.bfloat16)


def expert_grads(recv_ref, up_ref, down_ref, grad_up_ref, grad_down_ref, dot_ref, hid_ref, pre_ref):
    total, width = recv_ref.shape
    hidden_width = up_ref.shape[1]
    step = min(256, total)
    for r in range(total // step):
        at = slice(r * step, (r + 1) * step)
        block = recv_ref[at, :]
        preact = contract(block, up_ref[...], ((1,), (0,)))
        backprop = contract(block, down_ref[...], ((1,), (1,)))
        backprop = pltpu.roll(backprop, step - SLOTS, 0)
        lower = lax.broadcasted_iota(jnp.int32, (step, hidden_width), 0) % CHUNK < SLOTS
        sigma = jax.nn.sigmoid(preact)
        hidden = jnp.where(lower, preact * sigma, 0.0).astype(jnp.bfloat16).astype(jnp.float32)
        grad_pre = backprop * sigma * (1.0 + preact * (1.0 - sigma))
        pre_ref[at, :] = jnp.where(lower, grad_pre, 0.0).astype(jnp.bfloat16)
        hid_ref[at, :] = pltpu.roll(hidden, SLOTS, 0).astype(jnp.bfloat16)
        dots = jnp.sum(hidden * backprop, axis=1, keepdims=True)
        lane = lax.broadcasted_iota(jnp.int32, (step, 128), 1)
        sub = lax.broadcasted_iota(jnp.int32, (step, 128), 0) % CHUNK
        spread = jnp.where(lane == sub, dots, 0.0).reshape(step // CHUNK, CHUNK, 128)
        dot_ref[r * (step // CHUNK) : (r + 1) * (step // CHUNK), :] = jnp.sum(spread, axis=1)
    wide = min(512, width)
    for c in range(width // wide):
        at = slice(c * wide, (c + 1) * wide)
        grad_up_ref[at, :] = contract(recv_ref[:, at], pre_ref[...], ((0,), (0,))).astype(jnp.bfloat16)
        grad_down_ref[:, at] = contract(hid_ref[...], recv_ref[:, at], ((0,), (0,))).astype(jnp.bfloat16)


def gate_back(back_ref, code_ref, ids_ref, gates_ref, out_ref):
    count, experts = code_ref.shape
    back = back_ref[...].T
    code = code_ref[...]
    value = jnp.zeros((count, experts), jnp.float32)
    for j in range(SLOTS):
        value = jnp.where(code == float(j), back[j : j + 1, :], value)
    lane = lax.broadcasted_iota(jnp.int32, (count, experts), 1)
    for k in range(ids_ref.shape[1]):
        hit = ids_ref[:, k : k + 1] == lane
        total = jnp.sum(jnp.where(hit, value, 0.0), axis=1, keepdims=True)
        out_ref[:, k : k + 1] = total / gates_ref[:, k : k + 1].astype(jnp.float32)


VMEM = pl.BlockSpec(memory_space=pltpu.VMEM)
SMEM = pl.BlockSpec(memory_space=pltpu.SMEM)


def shards(tokens, cotangent, gate_values, expert_ids, hot_plan, expert_caps, w_up, w_down):
    experts = lax.axis_size("expert")
    count, width = tokens.shape
    hidden_width = w_up.shape[2]
    odd = (lax.axis_index("expert") % 2).astype(jnp.int32).reshape(1)
    sent, code = pl.pallas_call(
        route_pack,
        out_shape=(
            jax.ShapeDtypeStruct((experts * CHUNK, width), jnp.bfloat16),
            jax.ShapeDtypeStruct((count, experts), jnp.float32),
        ),
        in_specs=[SMEM] + [VMEM] * 6,
        out_specs=(VMEM, VMEM),
        compiler_params=pltpu.CompilerParams(vmem_limit_bytes=48 << 20),
    )(odd, expert_ids, gate_values, hot_plan.reshape(1, -1), expert_caps.reshape(1, -1), tokens, cotangent)
    recv = lax.all_to_all(
        sent.reshape(experts, CHUNK, width), "expert", split_axis=0, concat_axis=0, tiled=True
    )
    grad_up, grad_down, dots = pl.pallas_call(
        expert_grads,
        out_shape=(
            jax.ShapeDtypeStruct((width, hidden_width), jnp.bfloat16),
            jax.ShapeDtypeStruct((hidden_width, width), jnp.bfloat16),
            jax.ShapeDtypeStruct((experts, 128), jnp.float32),
        ),
        in_specs=[VMEM] * 3,
        out_specs=(VMEM,) * 3,
        scratch_shapes=[
            pltpu.VMEM((experts * CHUNK, hidden_width), jnp.bfloat16),
            pltpu.VMEM((experts * CHUNK, hidden_width), jnp.bfloat16),
        ],
        compiler_params=pltpu.CompilerParams(vmem_limit_bytes=48 << 20),
    )(recv.reshape(experts * CHUNK, width), w_up[0], w_down[0])
    summed_up = lax.psum_scatter(grad_up, "dp", scatter_dimension=0, tiled=True)
    summed_down = lax.psum_scatter(grad_down, "dp", scatter_dimension=1, tiled=True)
    back = lax.all_to_all(
        dots.reshape(experts, 1, 128), "expert", split_axis=0, concat_axis=0, tiled=True
    )
    gate_grad = pl.pallas_call(
        gate_back,
        out_shape=jax.ShapeDtypeStruct(gate_values.shape, jnp.float32),
        in_specs=[VMEM] * 4,
        out_specs=VMEM,
    )(back.reshape(experts, 128), code, expert_ids, gate_values)
    return summed_up[None], summed_down[None], gate_grad


def solution(mesh):
    rows = P(("dp", "expert"), None)
    return jax.shard_map(
        shards,
        mesh=mesh,
        in_specs=(rows, rows, rows, rows, P(), P(), P("expert", None, None), P("expert", None, None)),
        out_specs=(P("expert", "dp", None), P("expert", None, "dp"), rows),
        check_vma=False,
    )
```

```python
import jax
import jax.numpy as jnp
from jax import lax
from jax.experimental import pallas as pl
from jax.experimental.pallas import tpu as pltpu
from jax.sharding import PartitionSpec as P

SLOTS = 4
CHUNK = 2 * SLOTS
LANES = 128


def contract(a, b, dims):
    return lax.dot_general(a, b, (dims, ((), ())), preferred_element_type=jnp.float32)


def route_pack(
    odd_ref, ids_hbm, gates_hbm, hot_hbm, caps_hbm, x_hbm, dy_hbm, sent_hbm, code_ref,
    ids_ref, gates_ref, hot_ref, caps_ref, x_ref, dy_ref, sent_ref, sems,
):
    pairs = (
        (ids_hbm, ids_ref), (gates_hbm, gates_ref), (hot_hbm, hot_ref),
        (caps_hbm, caps_ref), (x_hbm, x_ref), (dy_hbm, dy_ref),
    )
    copies = [pltpu.make_async_copy(a, b, sems.at[i]) for i, (a, b) in enumerate(pairs)]
    for copy in copies:
        copy.start()
    top, count = ids_ref.shape
    experts = hot_ref.shape[1]
    wide = experts * CHUNK
    lane = lax.broadcasted_iota(jnp.int32, (count, experts), 1).astype(jnp.float32)
    row = lax.broadcasted_iota(jnp.int32, (count, count), 0)
    col = lax.broadcasted_iota(jnp.int32, (count, count), 1)
    below = (col < row).astype(jnp.bfloat16)
    eye = (col == row).astype(jnp.bfloat16)
    each = (
        lax.broadcasted_iota(jnp.int32, (top, top * experts), 1) // experts
        == lax.broadcasted_iota(jnp.int32, (top, top * experts), 0)
    ).astype(jnp.bfloat16)
    spread = (
        lax.broadcasted_iota(jnp.int32, (experts, wide), 1) // CHUNK
        == lax.broadcasted_iota(jnp.int32, (experts, wide), 0)
    ).astype(jnp.bfloat16)
    for copy in copies[:4]:
        copy.wait()
    ids = contract(ids_ref[...].astype(jnp.bfloat16), each, ((0,), (0,)))
    gates = contract(gates_ref[...], each, ((0,), (0,)))
    picked = jnp.zeros((count, experts), jnp.float32)
    place = jnp.zeros((count, experts), jnp.float32)
    gate = jnp.zeros((count, experts), jnp.float32)
    for k in range(top):
        at = slice(k * experts, (k + 1) * experts)
        hit = ids[:, at] == lane
        picked = jnp.where(hit, 1.0, picked)
        place = jnp.where(hit, float(k), place)
        gate = jnp.where(hit, gates[:, at], gate)
    rank = contract(below, picked.astype(jnp.bfloat16), ((1,), (0,)))
    admitted = jnp.where(rank < caps_ref[...].astype(jnp.float32), picked, 0.0)
    moves = hot_ref[...].astype(jnp.float32) * odd_ref[0].astype(jnp.float32)
    moved = admitted * moves
    stay = admitted - moved
    moved_next = pltpu.roll(moved, 1, 1)
    stay_next = pltpu.roll(stay, experts - 1, 1)
    before = contract(below, (stay + moved_next).astype(jnp.bfloat16), ((1,), (0,)))
    tie_stay = jnp.where(pltpu.roll(place, 1, 1) < place, moved_next, 0.0)
    tie_move = jnp.where(pltpu.roll(place, experts - 1, 1) < place, stay_next, 0.0)
    slot = jnp.where(moves > 0, pltpu.roll(before, experts - 1, 1) + tie_move, before + tie_stay)
    code = jnp.where((admitted > 0) & (slot < SLOTS), rank, -8.0).astype(jnp.bfloat16)
    code_ref[...] = contract(code, eye, ((0,), (0,)))
    part = lax.broadcasted_iota(jnp.int32, (count, wide), 1) % CHUNK
    code_wide = contract(code, spread, ((1,), (0,)))
    gate_wide = contract(gate.astype(jnp.bfloat16), spread, ((1,), (0,)))
    take_x = (code_wide == part.astype(jnp.float32)).astype(jnp.bfloat16)
    chosen = code_wide == (part - SLOTS).astype(jnp.float32)
    take_dy = chosen.astype(jnp.bfloat16)
    gate_pick = jnp.where(chosen, gate_wide, 0.0).astype(jnp.bfloat16)
    ones = jnp.ones((count, LANES), jnp.bfloat16)
    gate_col = contract(gate_pick, ones, ((0,), (0,)))
    gate_col = jnp.concatenate([gate_col] * 4, axis=1)
    step = gate_col.shape[1]
    for copy in copies[4:]:
        copy.wait()
    for c in range(x_ref.shape[1] // step):
        at = slice(c * step, (c + 1) * step)
        rows_x = contract(take_x, x_ref[:, at], ((0,), (0,)))
        rows_dy = contract(take_dy, dy_ref[:, at], ((0,), (0,)))
        sent_ref[:, at] = (rows_x + gate_col * rows_dy).astype(jnp.bfloat16)
        copies.append(pltpu.make_async_copy(sent_ref.at[:, at], sent_hbm.at[:, at], sems.at[6 + c]))
        copies[-1].start()
    for copy in copies[6:]:
        copy.wait()


def expert_down(
    recv_ref, up_ref, down_ref, grad_ref, dot_ref, x_ref, pre_ref, s_ref, hid_ref
):
    half, width = x_ref.shape
    step = half // 4
    lower = lax.broadcasted_iota(jnp.int32, (step, width), 0) % CHUNK < SLOTS
    lane = lax.broadcasted_iota(jnp.int32, (step, LANES), 1)
    sub = lax.broadcasted_iota(jnp.int32, (step, LANES), 0) % CHUNK
    for r in range(4):
        at = slice(r * step, (r + 1) * step)
        first = recv_ref[at, :]
        second = recv_ref[r * step + half : (r + 1) * step + half, :]
        x = jnp.where(lower, first, pltpu.roll(second, SLOTS, 0))
        s = jnp.where(lower, pltpu.roll(first, step - SLOTS, 0), second)
        x_ref[at, :] = x
        s_ref[at, :] = s
        preact = contract(x, up_ref[...], ((1,), (0,)))
        backprop = contract(s, down_ref[...], ((1,), (1,)))
        sigma = jax.nn.sigmoid(preact)
        hidden = (preact * sigma).astype(jnp.bfloat16)
        hid_ref[at, :] = hidden
        pre_ref[at, :] = (backprop * sigma * (1.0 + preact * (1.0 - sigma))).astype(jnp.bfloat16)
        dots = jnp.sum(hidden.astype(jnp.float32) * backprop, axis=1, keepdims=True)
        groups = step // CHUNK
        spread = jnp.where(lane == sub, dots, 0.0).reshape(groups, CHUNK, LANES)
        spread = jnp.sum(spread, axis=1)
        dot_ref[r * groups : (r + 1) * groups, :] = spread
        dot_ref[(r + 4) * groups : (r + 5) * groups, :] = pltpu.roll(spread, LANES - SLOTS, 1)
    parts = grad_ref.shape[0]
    wide = width // parts
    for c in range(parts):
        at = slice(c * wide, (c + 1) * wide)
        grad_ref[c] = contract(hid_ref[...], s_ref[:, at], ((0,), (0,))).astype(jnp.bfloat16)


def expert_up(me_ref, x_ref, pre_ref, own_ref, next_ref, last_ref, far_ref):
    wide = own_ref.shape[0]
    parts = x_ref.shape[1] // wide
    for shift, out in ((2, far_ref), (1, next_ref), (3, last_ref), (0, own_ref)):
        part = lax.rem(me_ref[0] + shift, parts)
        at = pl.ds(pl.multiple_of(part * wide, LANES), wide)
        out[...] = contract(x_ref[:, at], pre_ref[...], ((0,), (0,))).astype(jnp.bfloat16)


def gate_back(back_ref, code_ref, ids_ref, gates_ref, out_ref):
    experts, count = code_ref.shape
    code = code_ref[...]
    value = jnp.zeros((experts, count), jnp.float32)
    for j in range(SLOTS):
        value = jnp.where(code == float(j), back_ref[:, j : j + 1], value)
    row = lax.broadcasted_iota(jnp.int32, (experts, count), 0)
    for k in range(ids_ref.shape[0]):
        hit = row == ids_ref[k : k + 1, :]
        total = jnp.sum(jnp.where(hit, value, 0.0), axis=0, keepdims=True)
        out_ref[k : k + 1, :] = total / gates_ref[k : k + 1, :].astype(jnp.float32)


VMEM = pl.BlockSpec(memory_space=pltpu.VMEM)
SMEM = pl.BlockSpec(memory_space=pltpu.SMEM)
ANY = pl.BlockSpec(memory_space=pl.ANY)


def shards(tokens, cotangent, gate_values, expert_ids, hot_plan, expert_caps, w_up, w_down):
    experts = lax.axis_size("expert")
    groups = lax.axis_size("dp")
    count, width = tokens.shape
    top = gate_values.shape[1]
    hidden_width = w_up.shape[2]
    total = experts * CHUNK
    half = total // 2
    ids_t = expert_ids.T
    gates_t = gate_values.T
    odd = (lax.axis_index("expert") % 2).astype(jnp.int32).reshape(1)
    me = lax.axis_index("dp").astype(jnp.int32).reshape(1)
    whole = pltpu.CompilerParams(vmem_limit_bytes=56 << 20)
    part = pltpu.CompilerParams(vmem_limit_bytes=28 << 20)
    sent, code = pl.pallas_call(
        route_pack,
        out_shape=(
            jax.ShapeDtypeStruct((total, width), jnp.bfloat16),
            jax.ShapeDtypeStruct((experts, count), jnp.float32),
        ),
        in_specs=[SMEM] + [ANY] * 6,
        out_specs=(ANY, VMEM),
        scratch_shapes=[
            pltpu.VMEM((top, count), jnp.int32),
            pltpu.VMEM((top, count), jnp.bfloat16),
            pltpu.VMEM((1, experts), jnp.int32),
            pltpu.VMEM((1, experts), jnp.int32),
            pltpu.VMEM((count, width), jnp.bfloat16),
            pltpu.VMEM((count, width), jnp.bfloat16),
            pltpu.VMEM((total, width), jnp.bfloat16),
            pltpu.SemaphoreType.DMA((6 + width // 512,)),
        ],
        compiler_params=whole,
    )(odd, ids_t, gates_t, hot_plan.reshape(1, -1), expert_caps.reshape(1, -1), tokens, cotangent)
    recv = lax.all_to_all(
        sent.reshape(experts, CHUNK, width), "expert", split_axis=0, concat_axis=0, tiled=True
    )
    grad_down, dots, rows_x, grad_pre = pl.pallas_call(
        expert_down,
        out_shape=(
            jax.ShapeDtypeStruct((groups, hidden_width, width // groups), jnp.bfloat16),
            jax.ShapeDtypeStruct((experts, LANES), jnp.float32),
            jax.ShapeDtypeStruct((half, width), jnp.bfloat16),
            jax.ShapeDtypeStruct((half, hidden_width), jnp.bfloat16),
        ),
        in_specs=[VMEM] * 3,
        out_specs=(VMEM,) * 4,
        scratch_shapes=[
            pltpu.VMEM((half, width), jnp.bfloat16),
            pltpu.VMEM((half, hidden_width), jnp.bfloat16),
        ],
        compiler_params=part,
    )(recv.reshape(total, width), w_up[0], w_down[0])
    summed_down = lax.psum_scatter(
        grad_down.reshape(groups * hidden_width, -1), "dp", scatter_dimension=0, tiled=True
    )
    piece = jax.ShapeDtypeStruct((width // groups, hidden_width), jnp.bfloat16)
    own, ahead, behind, far = pl.pallas_call(
        expert_up,
        out_shape=(piece,) * 4,
        in_specs=[SMEM, VMEM, VMEM],
        out_specs=(VMEM,) * 4,
        compiler_params=part,
    )(me, rows_x, grad_pre)

    def shift(block, distance):
        return lax.ppermute(block, "dp", [(i, (i + distance) % groups) for i in range(groups)])

    far, ahead, behind = shift(far, 2), shift(ahead, 1), shift(behind, 3)
    summed_up = own.astype(jnp.float32) + far.astype(jnp.float32)
    summed_up = summed_up + ahead.astype(jnp.float32) + behind.astype(jnp.float32)
    back = lax.all_to_all(
        dots.reshape(experts, 1, LANES), "expert", split_axis=0, concat_axis=0, tiled=True
    )
    gate_grad = pl.pallas_call(
        gate_back,
        out_shape=jax.ShapeDtypeStruct((top, count), jnp.float32),
        in_specs=[VMEM] * 4,
        out_specs=VMEM,
    )(back.reshape(experts, LANES), code, ids_t, gates_t)
    return summed_up.astype(jnp.bfloat16)[None], summed_down[None], gate_grad.T


def solution(mesh):
    rows = P(("dp", "expert"), None)
    return jax.shard_map(
        shards,
        mesh=mesh,
        in_specs=(rows, rows, rows, rows, P(), P(), P("expert", None, None), P("expert", None, None)),
        out_specs=(P("expert", "dp", None), P("expert", None, "dp"), rows),
        check_vma=False,
    )
```

```python
import jax
import jax.numpy as jnp
from jax import lax
from jax.experimental import pallas as pl
from jax.experimental.pallas import tpu as pltpu
from jax.sharding import PartitionSpec as P

SLOTS = 4
CHUNK = 2 * SLOTS
LANES = 128


def contract(a, b, dims):
    return lax.dot_general(a, b, (dims, ((), ())), preferred_element_type=jnp.float32)


def route_pack(
    odd_ref, ids_hbm, gates_hbm, hot_hbm, caps_hbm, x_hbm, dy_hbm, sent_hbm, code_ref,
    ids_ref, gates_ref, hot_ref, caps_ref, x_ref, dy_ref, sent_ref, sems,
):
    pairs = (
        (ids_hbm, ids_ref), (gates_hbm, gates_ref), (hot_hbm, hot_ref),
        (caps_hbm, caps_ref), (x_hbm, x_ref), (dy_hbm, dy_ref),
    )
    copies = [pltpu.make_async_copy(a, b, sems.at[i]) for i, (a, b) in enumerate(pairs)]
    for copy in copies:
        copy.start()
    top, count = ids_ref.shape
    experts = hot_ref.shape[1]
    wide = experts * CHUNK
    lane = lax.broadcasted_iota(jnp.int32, (count, experts), 1).astype(jnp.float32)
    row = lax.broadcasted_iota(jnp.int32, (count, count), 0)
    col = lax.broadcasted_iota(jnp.int32, (count, count), 1)
    below = (col < row).astype(jnp.bfloat16)
    eye = (col == row).astype(jnp.bfloat16)
    each = (
        lax.broadcasted_iota(jnp.int32, (top, top * experts), 1) // experts
        == lax.broadcasted_iota(jnp.int32, (top, top * experts), 0)
    ).astype(jnp.bfloat16)
    spread = (
        lax.broadcasted_iota(jnp.int32, (experts, wide), 1) // CHUNK
        == lax.broadcasted_iota(jnp.int32, (experts, wide), 0)
    ).astype(jnp.bfloat16)
    for copy in copies[:4]:
        copy.wait()
    ids = contract(ids_ref[...].astype(jnp.bfloat16), each, ((0,), (0,)))
    gates = contract(gates_ref[...], each, ((0,), (0,)))
    picked = jnp.zeros((count, experts), jnp.float32)
    place = jnp.zeros((count, experts), jnp.float32)
    gate = jnp.zeros((count, experts), jnp.float32)
    for k in range(top):
        at = slice(k * experts, (k + 1) * experts)
        hit = ids[:, at] == lane
        picked = jnp.where(hit, 1.0, picked)
        place = jnp.where(hit, float(k), place)
        gate = jnp.where(hit, gates[:, at], gate)
    rank = contract(below, picked.astype(jnp.bfloat16), ((1,), (0,)))
    admitted = jnp.where(rank < caps_ref[...].astype(jnp.float32), picked, 0.0)
    moves = hot_ref[...].astype(jnp.float32) * odd_ref[0].astype(jnp.float32)
    moved = admitted * moves
    stay = admitted - moved
    moved_next = pltpu.roll(moved, 1, 1)
    stay_next = pltpu.roll(stay, experts - 1, 1)
    before = contract(below, (stay + moved_next).astype(jnp.bfloat16), ((1,), (0,)))
    tie_stay = jnp.where(pltpu.roll(place, 1, 1) < place, moved_next, 0.0)
    tie_move = jnp.where(pltpu.roll(place, experts - 1, 1) < place, stay_next, 0.0)
    slot = jnp.where(moves > 0, pltpu.roll(before, experts - 1, 1) + tie_move, before + tie_stay)
    code = jnp.where((admitted > 0) & (slot < SLOTS), rank, -8.0).astype(jnp.bfloat16)
    code_ref[...] = contract(code, eye, ((0,), (0,)))
    part = lax.broadcasted_iota(jnp.int32, (count, wide), 1) % CHUNK
    code_wide = contract(code, spread, ((1,), (0,)))
    gate_wide = contract(gate.astype(jnp.bfloat16), spread, ((1,), (0,)))
    take_x = (code_wide == part.astype(jnp.float32)).astype(jnp.bfloat16)
    chosen = code_wide == (part - SLOTS).astype(jnp.float32)
    take_dy = chosen.astype(jnp.bfloat16)
    gate_pick = jnp.where(chosen, gate_wide, 0.0).astype(jnp.bfloat16)
    ones = jnp.ones((count, LANES), jnp.bfloat16)
    gate_col = contract(gate_pick, ones, ((0,), (0,)))
    gate_col = jnp.concatenate([gate_col] * 4, axis=1)
    step = gate_col.shape[1]
    for copy in copies[4:]:
        copy.wait()
    for c in range(x_ref.shape[1] // step):
        at = slice(c * step, (c + 1) * step)
        rows_x = contract(take_x, x_ref[:, at], ((0,), (0,)))
        rows_dy = contract(take_dy, dy_ref[:, at], ((0,), (0,)))
        sent_ref[:, at] = (rows_x + gate_col * rows_dy).astype(jnp.bfloat16)
        copies.append(pltpu.make_async_copy(sent_ref.at[:, at], sent_hbm.at[:, at], sems.at[6 + c]))
        copies[-1].start()
    for copy in copies[6:]:
        copy.wait()


def write_piece(part, x_ref, s_ref, hid_ref, pre_ref, out_ref):
    parts = x_ref.shape[1] * pre_ref.shape[1] * 2 // (out_ref.shape[0] * LANES)
    wide = x_ref.shape[1] // parts
    tall = pre_ref.shape[1]
    at = pl.ds(pl.multiple_of(part * wide, LANES), wide)
    up = contract(x_ref[:, at], pre_ref[...], ((0,), (0,))).astype(jnp.bfloat16)
    for c in range(tall // LANES):
        out_ref[c * wide : (c + 1) * wide, :] = up[:, c * LANES : (c + 1) * LANES]
    down = contract(hid_ref[...], s_ref[:, at], ((0,), (0,))).astype(jnp.bfloat16)
    base = wide * tall // LANES
    for c in range(wide // LANES):
        out_ref[base + c * tall : base + (c + 1) * tall, :] = down[:, c * LANES : (c + 1) * LANES]


def expert_rows(
    me_ref, recv_hbm, up_ref, down_ref, own_ref, ahead_ref, behind_ref, far_ref, dot_ref,
    recv_ref, x_ref, s_ref, hid_ref, pre_ref, sems,
):
    half, width = x_ref.shape
    step = half // 4
    copies = []
    for n in range(8):
        at = pl.ds((n // 2) * step + (n % 2) * half, step)
        copies.append(pltpu.make_async_copy(recv_hbm.at[at, :], recv_ref.at[at, :], sems.at[n]))
        copies[-1].start()
    lower = lax.broadcasted_iota(jnp.int32, (step, width), 0) % CHUNK < SLOTS
    lane = lax.broadcasted_iota(jnp.int32, (step, LANES), 1)
    sub = lax.broadcasted_iota(jnp.int32, (step, LANES), 0) % CHUNK
    for r in range(4):
        at = slice(r * step, (r + 1) * step)
        copies[2 * r].wait()
        copies[2 * r + 1].wait()
        first = recv_ref[at, :]
        second = recv_ref[r * step + half : (r + 1) * step + half, :]
        x = jnp.where(lower, first, pltpu.roll(second, SLOTS, 0))
        s = jnp.where(lower, pltpu.roll(first, step - SLOTS, 0), second)
        x_ref[at, :] = x
        s_ref[at, :] = s
        preact = contract(x, up_ref[...], ((1,), (0,)))
        backprop = contract(s, down_ref[...], ((1,), (1,)))
        sigma = jax.nn.sigmoid(preact)
        hidden = (preact * sigma).astype(jnp.bfloat16)
        hid_ref[at, :] = hidden
        pre_ref[at, :] = (backprop * sigma * (1.0 + preact * (1.0 - sigma))).astype(jnp.bfloat16)
        dots = jnp.sum(hidden.astype(jnp.float32) * backprop, axis=1, keepdims=True)
        groups = step // CHUNK
        spread = jnp.where(lane == sub, dots, 0.0).reshape(groups, CHUNK, LANES)
        spread = jnp.sum(spread, axis=1)
        dot_ref[r * groups : (r + 1) * groups, :] = spread
        dot_ref[(r + 4) * groups : (r + 5) * groups, :] = pltpu.roll(spread, LANES - SLOTS, 1)
    parts = width * pre_ref.shape[1] * 2 // (own_ref.shape[0] * LANES)
    for shift, out_ref in ((2, far_ref), (1, ahead_ref), (3, behind_ref), (0, own_ref)):
        write_piece(lax.rem(me_ref[0] + shift, parts), x_ref, s_ref, hid_ref, pre_ref, out_ref)


def add_pieces(own_ref, far_ref, ahead_ref, behind_ref, up_ref, down_ref):
    refs = (own_ref, far_ref, ahead_ref, behind_ref)
    wide, tall = up_ref.shape
    base = wide * tall // LANES

    def total(at):
        first, second, third, fourth = [ref[at, :].astype(jnp.float32) for ref in refs]
        return ((first + second) + (third + fourth)).astype(jnp.bfloat16)

    for c in range(tall // LANES):
        up_ref[:, c * LANES : (c + 1) * LANES] = total(slice(c * wide, (c + 1) * wide))
    for c in range(wide // LANES):
        down_ref[:, c * LANES : (c + 1) * LANES] = total(slice(base + c * tall, base + (c + 1) * tall))


def gate_back(back_ref, code_ref, ids_ref, gates_ref, out_ref):
    experts, count = code_ref.shape
    code = code_ref[...]
    value = jnp.zeros((experts, count), jnp.float32)
    for j in range(SLOTS):
        value = jnp.where(code == float(j), back_ref[:, j : j + 1], value)
    row = lax.broadcasted_iota(jnp.int32, (experts, count), 0)
    for k in range(ids_ref.shape[0]):
        hit = row == ids_ref[k : k + 1, :]
        total = jnp.sum(jnp.where(hit, value, 0.0), axis=0, keepdims=True)
        out_ref[k : k + 1, :] = total / gates_ref[k : k + 1, :].astype(jnp.float32)


VMEM = pl.BlockSpec(memory_space=pltpu.VMEM)
SMEM = pl.BlockSpec(memory_space=pltpu.SMEM)
ANY = pl.BlockSpec(memory_space=pl.ANY)


def shards(tokens, cotangent, gate_values, expert_ids, hot_plan, expert_caps, w_up, w_down):
    experts = lax.axis_size("expert")
    groups = lax.axis_size("dp")
    count, width = tokens.shape
    top = gate_values.shape[1]
    hidden_width = w_up.shape[2]
    total = experts * CHUNK
    half = total // 2
    ids_t = expert_ids.T
    gates_t = gate_values.T
    odd = (lax.axis_index("expert") % 2).astype(jnp.int32).reshape(1)
    me = lax.axis_index("dp").astype(jnp.int32).reshape(1)
    whole = pltpu.CompilerParams(vmem_limit_bytes=56 << 20)
    part = pltpu.CompilerParams(vmem_limit_bytes=24 << 20)
    sent, code = pl.pallas_call(
        route_pack,
        out_shape=(
            jax.ShapeDtypeStruct((total, width), jnp.bfloat16),
            jax.ShapeDtypeStruct((experts, count), jnp.float32),
        ),
        in_specs=[SMEM] + [ANY] * 6,
        out_specs=(ANY, VMEM),
        scratch_shapes=[
            pltpu.VMEM((top, count), jnp.int32),
            pltpu.VMEM((top, count), jnp.bfloat16),
            pltpu.VMEM((1, experts), jnp.int32),
            pltpu.VMEM((1, experts), jnp.int32),
            pltpu.VMEM((count, width), jnp.bfloat16),
            pltpu.VMEM((count, width), jnp.bfloat16),
            pltpu.VMEM((total, width), jnp.bfloat16),
            pltpu.SemaphoreType.DMA((6 + width // 512,)),
        ],
        compiler_params=whole,
    )(odd, ids_t, gates_t, hot_plan.reshape(1, -1), expert_caps.reshape(1, -1), tokens, cotangent)
    recv = lax.all_to_all(
        sent.reshape(experts, CHUNK, width), "expert", split_axis=0, concat_axis=0, tiled=True
    )
    wide = width // groups
    piece = jax.ShapeDtypeStruct((2 * wide * hidden_width // LANES, LANES), jnp.bfloat16)
    own, ahead, behind, far, dots = pl.pallas_call(
        expert_rows,
        out_shape=(piece,) * 4 + (jax.ShapeDtypeStruct((experts, LANES), jnp.float32),),
        in_specs=[SMEM, ANY, VMEM, VMEM],
        out_specs=(VMEM,) * 5,
        scratch_shapes=[
            pltpu.VMEM((total, width), jnp.bfloat16),
            pltpu.VMEM((half, width), jnp.bfloat16),
            pltpu.VMEM((half, width), jnp.bfloat16),
            pltpu.VMEM((half, hidden_width), jnp.bfloat16),
            pltpu.VMEM((half, hidden_width), jnp.bfloat16),
            pltpu.SemaphoreType.DMA((8,)),
        ],
        compiler_params=part,
    )(me, recv.reshape(total, width), w_up[0], w_down[0])

    def shift(block, distance):
        return lax.ppermute(block, "dp", [(i, (i + distance) % groups) for i in range(groups)])

    far, ahead, behind = shift(far, 2), shift(ahead, 1), shift(behind, 3)
    summed_up, summed_down = pl.pallas_call(
        add_pieces,
        out_shape=(
            jax.ShapeDtypeStruct((wide, hidden_width), jnp.bfloat16),
            jax.ShapeDtypeStruct((hidden_width, wide), jnp.bfloat16),
        ),
        in_specs=[VMEM] * 4,
        out_specs=(VMEM,) * 2,
        compiler_params=pltpu.CompilerParams(vmem_limit_bytes=12 << 20),
    )(own, far, ahead, behind)
    back = lax.all_to_all(
        dots.reshape(experts, 1, LANES), "expert", split_axis=0, concat_axis=0, tiled=True
    )
    gate_grad = pl.pallas_call(
        gate_back,
        out_shape=jax.ShapeDtypeStruct((top, count), jnp.float32),
        compiler_params=pltpu.CompilerParams(vmem_limit_bytes=8 << 20),
        in_specs=[VMEM] * 4,
        out_specs=VMEM,
    )(back.reshape(experts, LANES), code, ids_t, gates_t)
    return summed_up[None], summed_down[None], gate_grad.T


def solution(mesh):
    rows = P(("dp", "expert"), None)
    return jax.shard_map(
        shards,
        mesh=mesh,
        in_specs=(rows, rows, rows, rows, P(), P(), P("expert", None, None), P("expert", None, None)),
        out_specs=(P("expert", "dp", None), P("expert", None, "dp"), rows),
        check_vma=False,
    )
```

```python
import jax
import jax.numpy as jnp
from jax import lax
from jax.experimental import pallas as pl
from jax.experimental.pallas import tpu as pltpu
from jax.sharding import PartitionSpec as P

SLOTS = 4
CHUNK = 2 * SLOTS
LANES = 128


def contract(a, b, dims):
    return lax.dot_general(a, b, (dims, ((), ())), preferred_element_type=jnp.float32)


def route_pack(
    place_ref, ids_hbm, gates_hbm, hot_hbm, caps_hbm, x_hbm, dy_hbm, sent_hbm, code_ref,
    ids_ref, gates_ref, hot_ref, caps_ref, x_ref, dy_ref, sent_ref, sems,
):
    pairs = (
        (ids_hbm, ids_ref), (gates_hbm, gates_ref), (hot_hbm, hot_ref),
        (caps_hbm, caps_ref), (x_hbm, x_ref), (dy_hbm, dy_ref),
    )
    copies = [pltpu.make_async_copy(a, b, sems.at[i]) for i, (a, b) in enumerate(pairs)]
    for copy in copies:
        copy.start()
    top, count = ids_ref.shape
    experts = hot_ref.shape[1]
    wide = experts * CHUNK
    lane = lax.broadcasted_iota(jnp.int32, (count, experts), 1).astype(jnp.float32)
    row = lax.broadcasted_iota(jnp.int32, (count, count), 0)
    col = lax.broadcasted_iota(jnp.int32, (count, count), 1)
    below = (col < row).astype(jnp.bfloat16)
    eye = (col == row).astype(jnp.bfloat16)
    each = (
        lax.broadcasted_iota(jnp.int32, (top, top * experts), 1) // experts
        == lax.broadcasted_iota(jnp.int32, (top, top * experts), 0)
    ).astype(jnp.bfloat16)
    spread = (
        lax.broadcasted_iota(jnp.int32, (experts, wide), 1) // CHUNK
        == lax.broadcasted_iota(jnp.int32, (experts, wide), 0)
    ).astype(jnp.bfloat16)
    for copy in copies[:4]:
        copy.wait()
    ids = contract(ids_ref[...].astype(jnp.bfloat16), each, ((0,), (0,)))
    gates = contract(gates_ref[...], each, ((0,), (0,)))
    picked = jnp.zeros((count, experts), jnp.float32)
    place = jnp.zeros((count, experts), jnp.float32)
    gate = jnp.zeros((count, experts), jnp.float32)
    for k in range(top):
        at = slice(k * experts, (k + 1) * experts)
        hit = ids[:, at] == lane
        picked = jnp.where(hit, 1.0, picked)
        place = jnp.where(hit, float(k), place)
        gate = jnp.where(hit, gates[:, at], gate)
    rank = contract(below, picked.astype(jnp.bfloat16), ((1,), (0,)))
    admitted = jnp.where(rank < caps_ref[...].astype(jnp.float32), picked, 0.0)
    moves = hot_ref[...].astype(jnp.float32) * place_ref[1].astype(jnp.float32)
    moved = admitted * moves
    stay = admitted - moved
    moved_next = pltpu.roll(moved, 1, 1)
    stay_next = pltpu.roll(stay, experts - 1, 1)
    before = contract(below, (stay + moved_next).astype(jnp.bfloat16), ((1,), (0,)))
    tie_stay = jnp.where(pltpu.roll(place, 1, 1) < place, moved_next, 0.0)
    tie_move = jnp.where(pltpu.roll(place, experts - 1, 1) < place, stay_next, 0.0)
    slot = jnp.where(moves > 0, pltpu.roll(before, experts - 1, 1) + tie_move, before + tie_stay)
    code = jnp.where((admitted > 0) & (slot < SLOTS), rank, -8.0).astype(jnp.bfloat16)
    code_ref[...] = contract(code, eye, ((0,), (0,)))
    part = lax.broadcasted_iota(jnp.int32, (count, wide), 1) % CHUNK
    code_wide = contract(code, spread, ((1,), (0,)))
    gate_wide = contract(gate.astype(jnp.bfloat16), spread, ((1,), (0,)))
    take_x = (code_wide == part.astype(jnp.float32)).astype(jnp.bfloat16)
    chosen = code_wide == (part - SLOTS).astype(jnp.float32)
    take_dy = chosen.astype(jnp.bfloat16)
    gate_pick = jnp.where(chosen, gate_wide, 0.0).astype(jnp.bfloat16)
    ones = jnp.ones((count, LANES), jnp.bfloat16)
    gate_col = contract(gate_pick, ones, ((0,), (0,)))
    gate_col = jnp.concatenate([gate_col] * 4, axis=1)
    step = gate_col.shape[1]
    for copy in copies[4:]:
        copy.wait()
    for c in range(x_ref.shape[1] // step):
        at = slice(c * step, (c + 1) * step)
        rows_x = contract(take_x, x_ref[:, at], ((0,), (0,)))
        rows_dy = contract(take_dy, dy_ref[:, at], ((0,), (0,)))
        sent_ref[:, at] = (rows_x + gate_col * rows_dy).astype(jnp.bfloat16)
        copies.append(pltpu.make_async_copy(sent_ref.at[:, at], sent_hbm.at[:, at], sems.at[6 + c]))
        copies[-1].start()
    for copy in copies[6:]:
        copy.wait()


def write_piece(part, x_ref, s_ref, hid_ref, pre_ref, out_ref):
    parts = x_ref.shape[1] * pre_ref.shape[1] * 2 // (out_ref.shape[0] * LANES)
    wide = x_ref.shape[1] // parts
    tall = pre_ref.shape[1]
    at = pl.ds(pl.multiple_of(part * wide, LANES), wide)
    up = contract(x_ref[:, at], pre_ref[...], ((0,), (0,))).astype(jnp.bfloat16)
    for c in range(tall // LANES):
        out_ref[c * wide : (c + 1) * wide, :] = up[:, c * LANES : (c + 1) * LANES]
    down = contract(hid_ref[...], s_ref[:, at], ((1,), (0,))).astype(jnp.bfloat16)
    base = wide * tall // LANES
    for c in range(wide // LANES):
        out_ref[base + c * tall : base + (c + 1) * tall, :] = down[:, c * LANES : (c + 1) * LANES]


def expert_rows(
    place_ref, recv_ref, up_ref, down_ref, own_ref, ahead_ref, behind_ref, far_ref, dot_ref,
    x_ref, s_ref, hid_ref, pre_ref,
):
    half, width = x_ref.shape
    step = half // 4
    lower = lax.broadcasted_iota(jnp.int32, (step, width), 0) % CHUNK < SLOTS
    lane = lax.broadcasted_iota(jnp.int32, (step, LANES), 1)
    sub = lax.broadcasted_iota(jnp.int32, (step, LANES), 0) % CHUNK
    for r in range(4):
        at = slice(r * step, (r + 1) * step)
        first = recv_ref[at, :]
        second = recv_ref[r * step + half : (r + 1) * step + half, :]
        x = jnp.where(lower, first, pltpu.roll(second, SLOTS, 0))
        s = jnp.where(lower, pltpu.roll(first, step - SLOTS, 0), second)
        x_ref[at, :] = x
        s_ref[at, :] = s
        preact = contract(x, up_ref[...], ((1,), (0,)))
        backprop = contract(s, down_ref[...], ((1,), (1,)))
        sigma = jax.nn.sigmoid(preact)
        hidden = (preact * sigma).astype(jnp.bfloat16)
        hid_ref[:, at] = hidden.T
        pre_ref[at, :] = (backprop * sigma * (1.0 + preact * (1.0 - sigma))).astype(jnp.bfloat16)
        dots = jnp.sum(hidden.astype(jnp.float32) * backprop, axis=1, keepdims=True)
        groups = step // CHUNK
        spread = jnp.where(lane == sub, dots, 0.0).reshape(groups, CHUNK, LANES)
        spread = jnp.sum(spread, axis=1)
        dot_ref[r * groups : (r + 1) * groups, :] = spread
        dot_ref[(r + 4) * groups : (r + 5) * groups, :] = pltpu.roll(spread, LANES - SLOTS, 1)
    parts = width * pre_ref.shape[1] * 2 // (own_ref.shape[0] * LANES)
    for shift, out_ref in ((2, far_ref), (1, ahead_ref), (3, behind_ref), (0, own_ref)):
        write_piece(lax.rem(place_ref[0] + shift, parts), x_ref, s_ref, hid_ref, pre_ref, out_ref)


def add_pieces(own_ref, far_ref, ahead_ref, behind_ref, up_ref, down_ref):
    refs = (own_ref, far_ref, ahead_ref, behind_ref)
    wide, tall = up_ref.shape
    base = wide * tall // LANES

    def total(at):
        first, second, third, fourth = [ref[at, :].astype(jnp.float32) for ref in refs]
        return ((first + second) + (third + fourth)).astype(jnp.bfloat16)

    for c in range(tall // LANES):
        up_ref[:, c * LANES : (c + 1) * LANES] = total(slice(c * wide, (c + 1) * wide))
    for c in range(wide // LANES):
        down_ref[:, c * LANES : (c + 1) * LANES] = total(slice(base + c * tall, base + (c + 1) * tall))


def gate_back(back_ref, code_ref, ids_ref, gates_ref, out_ref):
    experts, count = code_ref.shape
    code = code_ref[...]
    value = jnp.zeros((experts, count), jnp.float32)
    for j in range(SLOTS):
        value = jnp.where(code == float(j), back_ref[:, j : j + 1], value)
    row = lax.broadcasted_iota(jnp.int32, (experts, count), 0)
    for k in range(ids_ref.shape[0]):
        hit = row == ids_ref[k : k + 1, :]
        total = jnp.sum(jnp.where(hit, value, 0.0), axis=0, keepdims=True)
        out_ref[k : k + 1, :] = total / gates_ref[k : k + 1, :].astype(jnp.float32)


VMEM = pl.BlockSpec(memory_space=pltpu.VMEM)
SMEM = pl.BlockSpec(memory_space=pltpu.SMEM)
ANY = pl.BlockSpec(memory_space=pl.ANY)


def shards(tokens, cotangent, gate_values, expert_ids, hot_plan, expert_caps, w_up, w_down):
    experts = lax.axis_size("expert")
    groups = lax.axis_size("dp")
    count, width = tokens.shape
    top = gate_values.shape[1]
    hidden_width = w_up.shape[2]
    total = experts * CHUNK
    half = total // 2
    ids_t = expert_ids.T
    gates_t = gate_values.T
    place = jnp.stack([lax.axis_index("dp"), lax.axis_index("expert") % 2]).astype(jnp.int32)
    whole = pltpu.CompilerParams(vmem_limit_bytes=56 << 20)
    part = pltpu.CompilerParams(vmem_limit_bytes=24 << 20)
    sent, code = pl.pallas_call(
        route_pack,
        out_shape=(
            jax.ShapeDtypeStruct((total, width), jnp.bfloat16),
            jax.ShapeDtypeStruct((experts, count), jnp.float32),
        ),
        in_specs=[SMEM] + [ANY] * 6,
        out_specs=(ANY, VMEM),
        scratch_shapes=[
            pltpu.VMEM((top, count), jnp.int32),
            pltpu.VMEM((top, count), jnp.bfloat16),
            pltpu.VMEM((1, experts), jnp.int32),
            pltpu.VMEM((1, experts), jnp.int32),
            pltpu.VMEM((count, width), jnp.bfloat16),
            pltpu.VMEM((count, width), jnp.bfloat16),
            pltpu.VMEM((total, width), jnp.bfloat16),
            pltpu.SemaphoreType.DMA((6 + width // 512,)),
        ],
        compiler_params=whole,
    )(place, ids_t, gates_t, hot_plan.reshape(1, -1), expert_caps.reshape(1, -1), tokens, cotangent)
    recv = lax.all_to_all(
        sent.reshape(experts, CHUNK, width), "expert", split_axis=0, concat_axis=0, tiled=True
    )
    wide = width // groups
    piece = jax.ShapeDtypeStruct((2 * wide * hidden_width // LANES, LANES), jnp.bfloat16)
    own, ahead, behind, far, dots = pl.pallas_call(
        expert_rows,
        out_shape=(piece,) * 4 + (jax.ShapeDtypeStruct((experts, LANES), jnp.float32),),
        in_specs=[SMEM] + [VMEM] * 3,
        out_specs=(VMEM,) * 5,
        scratch_shapes=[
            pltpu.VMEM((half, width), jnp.bfloat16),
            pltpu.VMEM((half, width), jnp.bfloat16),
            pltpu.VMEM((hidden_width, half), jnp.bfloat16),
            pltpu.VMEM((half, hidden_width), jnp.bfloat16),
        ],
        compiler_params=part,
    )(place, recv.reshape(total, width), w_up[0], w_down[0])

    def shift(block, distance):
        return lax.ppermute(block, "dp", [(i, (i + distance) % groups) for i in range(groups)])

    far, ahead, behind = shift(far, 2), shift(ahead, 1), shift(behind, 3)
    summed_up, summed_down = pl.pallas_call(
        add_pieces,
        out_shape=(
            jax.ShapeDtypeStruct((wide, hidden_width), jnp.bfloat16),
            jax.ShapeDtypeStruct((hidden_width, wide), jnp.bfloat16),
        ),
        in_specs=[VMEM] * 4,
        out_specs=(VMEM,) * 2,
        compiler_params=pltpu.CompilerParams(vmem_limit_bytes=12 << 20),
    )(own, far, ahead, behind)
    back = lax.all_to_all(
        dots.reshape(experts, 1, LANES), "expert", split_axis=0, concat_axis=0, tiled=True
    )
    gate_grad = pl.pallas_call(
        gate_back,
        out_shape=jax.ShapeDtypeStruct((top, count), jnp.float32),
        compiler_params=pltpu.CompilerParams(vmem_limit_bytes=8 << 20),
        in_specs=[VMEM] * 4,
        out_specs=VMEM,
    )(back.reshape(experts, LANES), code, ids_t, gates_t)
    return summed_up[None], summed_down[None], gate_grad.T


def solution(mesh):
    rows = P(("dp", "expert"), None)
    return jax.shard_map(
        shards,
        mesh=mesh,
        in_specs=(rows, rows, rows, rows, P(), P(), P("expert", None, None), P("expert", None, None)),
        out_specs=(P("expert", "dp", None), P("expert", None, "dp"), rows),
        check_vma=False,
    )
```

```python
import jax
import jax.numpy as jnp
from jax import lax
from jax.experimental import pallas as pl
from jax.experimental.pallas import tpu as pltpu
from jax.sharding import PartitionSpec as P

SLOTS = 4
CHUNK = 2 * SLOTS
LANES = 128
STEPS = 1


def contract(a, b, dims):
    return lax.dot_general(a, b, (dims, ((), ())), preferred_element_type=jnp.float32)


def route_pack(
    me_ref, odd_ref, ids_hbm, gates_hbm, hot_hbm, caps_hbm, x_hbm, dy_hbm, sent_hbm, code_ref,
    ids_ref, gates_ref, hot_ref, caps_ref, rows_ref, sent_ref, sems,
):
    top, count = ids_ref.shape
    pairs = (
        (ids_hbm, ids_ref), (gates_hbm, gates_ref), (hot_hbm, hot_ref), (caps_hbm, caps_ref),
        (x_hbm, rows_ref.at[pl.ds(0, count), :]), (dy_hbm, rows_ref.at[pl.ds(count, count), :]),
    )
    copies = [pltpu.make_async_copy(a, b, sems.at[i]) for i, (a, b) in enumerate(pairs)]
    for copy in copies:
        copy.start()
    experts = hot_ref.shape[1]
    wide = experts * CHUNK
    lane = lax.broadcasted_iota(jnp.int32, (count, experts), 1).astype(jnp.float32)
    row = lax.broadcasted_iota(jnp.int32, (count, count), 0)
    col = lax.broadcasted_iota(jnp.int32, (count, count), 1)
    below = (col < row).astype(jnp.bfloat16)
    eye = (col == row).astype(jnp.bfloat16)
    each = (
        lax.broadcasted_iota(jnp.int32, (top, top * experts), 1) // experts
        == lax.broadcasted_iota(jnp.int32, (top, top * experts), 0)
    ).astype(jnp.bfloat16)
    spread = (
        lax.broadcasted_iota(jnp.int32, (experts, wide), 1) // CHUNK
        == lax.broadcasted_iota(jnp.int32, (experts, wide), 0)
    ).astype(jnp.bfloat16)
    for copy in copies[:4]:
        copy.wait()
    ids = contract(ids_ref[...].astype(jnp.bfloat16), each, ((0,), (0,)))
    gates = contract(gates_ref[...], each, ((0,), (0,)))
    picked = jnp.zeros((count, experts), jnp.float32)
    place = jnp.zeros((count, experts), jnp.float32)
    gate = jnp.zeros((count, experts), jnp.float32)
    for k in range(top):
        at = slice(k * experts, (k + 1) * experts)
        hit = ids[:, at] == lane
        picked = jnp.where(hit, 1.0, picked)
        place = jnp.where(hit, float(k), place)
        gate = jnp.where(hit, gates[:, at], gate)
    rank = contract(below, picked.astype(jnp.bfloat16), ((1,), (0,)))
    admitted = jnp.where(rank < caps_ref[...].astype(jnp.float32), picked, 0.0)
    moves = hot_ref[...].astype(jnp.float32) * odd_ref[0].astype(jnp.float32)
    moved = admitted * moves
    stay = admitted - moved
    moved_next = pltpu.roll(moved, 1, 1)
    stay_next = pltpu.roll(stay, experts - 1, 1)
    before = contract(below, (stay + moved_next).astype(jnp.bfloat16), ((1,), (0,)))
    tie_stay = jnp.where(pltpu.roll(place, 1, 1) < place, moved_next, 0.0)
    tie_move = jnp.where(pltpu.roll(place, experts - 1, 1) < place, stay_next, 0.0)
    slot = jnp.where(moves > 0, pltpu.roll(before, experts - 1, 1) + tie_move, before + tie_stay)
    code = jnp.where((admitted > 0) & (slot < SLOTS), rank, -8.0).astype(jnp.bfloat16)
    code_ref[...] = contract(code, eye, ((0,), (0,)))
    part = lax.broadcasted_iota(jnp.int32, (count, wide), 1) % CHUNK
    code_wide = contract(code, spread, ((1,), (0,)))
    gate_wide = contract(gate.astype(jnp.bfloat16), spread, ((1,), (0,)))
    chosen = code_wide == (part - SLOTS).astype(jnp.float32)
    take = jnp.concatenate([code_wide == part.astype(jnp.float32), chosen], axis=0).astype(jnp.bfloat16)
    gate_pick = jnp.where(chosen, gate_wide, 0.0).astype(jnp.bfloat16)
    ones = jnp.ones((count, LANES), jnp.bfloat16)
    scale = contract(gate_pick, ones, ((0,), (0,)))
    is_x = lax.broadcasted_iota(jnp.int32, (wide, LANES), 0) % CHUNK < SLOTS
    scale = jnp.where(is_x, 1.0, scale)
    scale = jnp.concatenate([scale] * 4, axis=1)
    step = scale.shape[1]
    for copy in copies[4:]:
        copy.wait()
    for c in range(rows_ref.shape[1] // step):
        at = slice(c * step, (c + 1) * step)
        rows = contract(take, rows_ref[:, at], ((0,), (0,)))
        sent_ref[:, at] = (rows * scale).astype(jnp.bfloat16)
        copies.append(pltpu.make_async_copy(sent_ref.at[:, at], sent_hbm.at[:, at], sems.at[6 + c]))
        copies[-1].start()
    for copy in copies[6:]:
        copy.wait()


def write_piece(part, x_ref, s_ref, hid_ref, pre_ref, out_ref):
    parts = x_ref.shape[1] * pre_ref.shape[1] * 2 // (out_ref.shape[0] * LANES)
    wide = x_ref.shape[1] // parts
    tall = pre_ref.shape[1]
    at = pl.ds(pl.multiple_of(part * wide, LANES), wide)
    up = contract(x_ref[:, at], pre_ref[...], ((0,), (0,))).astype(jnp.bfloat16)
    for c in range(tall // LANES):
        out_ref[c * wide : (c + 1) * wide, :] = up[:, c * LANES : (c + 1) * LANES]
    down = contract(hid_ref[...], s_ref[:, at], ((1,), (0,))).astype(jnp.bfloat16)
    base = wide * tall // LANES
    for c in range(wide // LANES):
        out_ref[base + c * tall : base + (c + 1) * tall, :] = down[:, c * LANES : (c + 1) * LANES]


def expert_rows(
    me_ref, recv_ref, up_ref, down_ref, own_ref, ahead_ref, behind_ref, far_ref, dot_ref,
    x_ref, s_ref, hid_ref, pre_ref,
):
    half, width = x_ref.shape
    step = half // STEPS
    lower = lax.broadcasted_iota(jnp.int32, (step, width), 0) % CHUNK < SLOTS
    lane = lax.broadcasted_iota(jnp.int32, (step, LANES), 1)
    sub = lax.broadcasted_iota(jnp.int32, (step, LANES), 0) % CHUNK
    for r in range(STEPS):
        at = slice(r * step, (r + 1) * step)
        first = recv_ref[at, :]
        second = recv_ref[r * step + half : (r + 1) * step + half, :]
        x = jnp.where(lower, first, pltpu.roll(second, SLOTS, 0))
        s = jnp.where(lower, pltpu.roll(first, step - SLOTS, 0), second)
        x_ref[at, :] = x
        s_ref[at, :] = s
        preact = contract(x, up_ref[...], ((1,), (0,)))
        backprop = contract(s, down_ref[...], ((1,), (1,)))
        sigma = jax.nn.sigmoid(preact)
        hidden = (preact * sigma).astype(jnp.bfloat16)
        hid_ref[:, at] = hidden.T
        pre_ref[at, :] = (backprop * sigma * (1.0 + preact * (1.0 - sigma))).astype(jnp.bfloat16)
        dots = jnp.sum(hidden.astype(jnp.float32) * backprop, axis=1, keepdims=True)
        groups = step // CHUNK
        spread = jnp.where(lane == sub, dots, 0.0).reshape(groups, CHUNK, LANES)
        spread = jnp.sum(spread, axis=1)
        dot_ref[r * groups : (r + 1) * groups, :] = spread
        dot_ref[(r + STEPS) * groups : (r + STEPS + 1) * groups, :] = pltpu.roll(spread, LANES - SLOTS, 1)
    parts = width * pre_ref.shape[1] * 2 // (own_ref.shape[0] * LANES)
    for shift, out_ref in ((2, far_ref), (1, ahead_ref), (3, behind_ref), (0, own_ref)):
        write_piece(lax.rem(me_ref[0] + shift, parts), x_ref, s_ref, hid_ref, pre_ref, out_ref)


def add_pieces(own_ref, far_ref, ahead_ref, behind_ref, up_ref, down_ref):
    refs = (own_ref, far_ref, ahead_ref, behind_ref)
    wide, tall = up_ref.shape
    base = wide * tall // LANES

    def total(at):
        first, second, third, fourth = [ref[at, :].astype(jnp.float32) for ref in refs]
        return ((first + second) + (third + fourth)).astype(jnp.bfloat16)

    for c in range(tall // LANES):
        up_ref[:, c * LANES : (c + 1) * LANES] = total(slice(c * wide, (c + 1) * wide))
    for c in range(wide // LANES):
        down_ref[:, c * LANES : (c + 1) * LANES] = total(slice(base + c * tall, base + (c + 1) * tall))


def gate_back(back_ref, code_ref, ids_ref, gates_ref, out_ref):
    experts, count = code_ref.shape
    code = code_ref[...]
    value = jnp.zeros((experts, count), jnp.float32)
    for j in range(SLOTS):
        value = jnp.where(code == float(j), back_ref[:, j : j + 1], value)
    row = lax.broadcasted_iota(jnp.int32, (experts, count), 0)
    for k in range(ids_ref.shape[0]):
        hit = row == ids_ref[k : k + 1, :]
        total = jnp.sum(jnp.where(hit, value, 0.0), axis=0, keepdims=True)
        out_ref[k : k + 1, :] = total / gates_ref[k : k + 1, :].astype(jnp.float32)


VMEM = pl.BlockSpec(memory_space=pltpu.VMEM)
SMEM = pl.BlockSpec(memory_space=pltpu.SMEM)
ANY = pl.BlockSpec(memory_space=pl.ANY)


def shards(tokens, cotangent, gate_values, expert_ids, hot_plan, expert_caps, w_up, w_down):
    experts = lax.axis_size("expert")
    groups = lax.axis_size("dp")
    count, width = tokens.shape
    top = gate_values.shape[1]
    hidden_width = w_up.shape[2]
    total = experts * CHUNK
    half = total // 2
    ids_t = expert_ids.T
    gates_t = gate_values.T
    me = lax.axis_index("dp").astype(jnp.int32).reshape(1)
    odd = (lax.axis_index("expert") % 2).astype(jnp.int32).reshape(1)
    whole = pltpu.CompilerParams(vmem_limit_bytes=56 << 20)
    part = pltpu.CompilerParams(vmem_limit_bytes=24 << 20)
    sent, code = pl.pallas_call(
        route_pack,
        out_shape=(
            jax.ShapeDtypeStruct((total, width), jnp.bfloat16),
            jax.ShapeDtypeStruct((experts, count), jnp.float32),
        ),
        in_specs=[SMEM, SMEM] + [ANY] * 6,
        out_specs=(ANY, VMEM),
        scratch_shapes=[
            pltpu.VMEM((top, count), jnp.int32),
            pltpu.VMEM((top, count), jnp.bfloat16),
            pltpu.VMEM((1, experts), jnp.int32),
            pltpu.VMEM((1, experts), jnp.int32),
            pltpu.VMEM((2 * count, width), jnp.bfloat16),
            pltpu.VMEM((total, width), jnp.bfloat16),
            pltpu.SemaphoreType.DMA((6 + width // 512,)),
        ],
        compiler_params=whole,
    )(me, odd, ids_t, gates_t, hot_plan.reshape(1, -1), expert_caps.reshape(1, -1), tokens, cotangent)
    recv = lax.all_to_all(
        sent.reshape(experts, CHUNK, width), "expert", split_axis=0, concat_axis=0, tiled=True
    )
    wide = width // groups
    piece = jax.ShapeDtypeStruct((2 * wide * hidden_width // LANES, LANES), jnp.bfloat16)
    own, ahead, behind, far, dots = pl.pallas_call(
        expert_rows,
        out_shape=(piece,) * 4 + (jax.ShapeDtypeStruct((experts, LANES), jnp.float32),),
        in_specs=[SMEM] + [VMEM] * 3,
        out_specs=(VMEM,) * 5,
        scratch_shapes=[
            pltpu.VMEM((half, width), jnp.bfloat16),
            pltpu.VMEM((half, width), jnp.bfloat16),
            pltpu.VMEM((hidden_width, half), jnp.bfloat16),
            pltpu.VMEM((half, hidden_width), jnp.bfloat16),
        ],
        compiler_params=part,
    )(me, recv.reshape(total, width), w_up[0], w_down[0])

    def shift(block, distance):
        return lax.ppermute(block, "dp", [(i, (i + distance) % groups) for i in range(groups)])

    far, ahead, behind = shift(far, 2), shift(ahead, 1), shift(behind, 3)
    summed_up, summed_down = pl.pallas_call(
        add_pieces,
        out_shape=(
            jax.ShapeDtypeStruct((wide, hidden_width), jnp.bfloat16),
            jax.ShapeDtypeStruct((hidden_width, wide), jnp.bfloat16),
        ),
        in_specs=[VMEM] * 4,
        out_specs=(VMEM,) * 2,
        compiler_params=pltpu.CompilerParams(vmem_limit_bytes=12 << 20),
    )(own, far, ahead, behind)
    back = lax.all_to_all(
        dots.reshape(experts, 1, LANES), "expert", split_axis=0, concat_axis=0, tiled=True
    )
    gate_grad = pl.pallas_call(
        gate_back,
        out_shape=jax.ShapeDtypeStruct((top, count), jnp.float32),
        compiler_params=pltpu.CompilerParams(vmem_limit_bytes=8 << 20),
        in_specs=[VMEM] * 4,
        out_specs=VMEM,
    )(back.reshape(experts, LANES), code, ids_t, gates_t)
    return summed_up[None], summed_down[None], gate_grad.T


def solution(mesh):
    rows = P(("dp", "expert"), None)
    return jax.shard_map(
        shards,
        mesh=mesh,
        in_specs=(rows, rows, rows, rows, P(), P(), P("expert", None, None), P("expert", None, None)),
        out_specs=(P("expert", "dp", None), P("expert", None, "dp"), rows),
        check_vma=False,
    )
```

```python
import jax
import jax.numpy as jnp
from jax import lax
from jax.experimental import pallas as pl
from jax.experimental.pallas import tpu as pltpu
from jax.sharding import PartitionSpec as P

SLOTS = 4
CHUNK = 2 * SLOTS
LANES = 128
STEPS = 1


def contract(a, b, dims):
    return lax.dot_general(a, b, (dims, ((), ())), preferred_element_type=jnp.float32)


def route_pack(
    me_ref, odd_ref, ids_hbm, gates_hbm, hot_hbm, caps_hbm, x_hbm, dy_hbm, sent_hbm, code_ref,
    ids_ref, gates_ref, hot_ref, caps_ref, rows_ref, sent_ref, sems,
):
    top, count = ids_ref.shape
    pairs = (
        (ids_hbm, ids_ref), (gates_hbm, gates_ref), (hot_hbm, hot_ref), (caps_hbm, caps_ref),
        (x_hbm, rows_ref.at[pl.ds(0, count), :]), (dy_hbm, rows_ref.at[pl.ds(count, count), :]),
    )
    copies = [pltpu.make_async_copy(a, b, sems.at[i]) for i, (a, b) in enumerate(pairs)]
    for copy in copies:
        copy.start()
    experts = hot_ref.shape[1]
    wide = experts * CHUNK
    lane = lax.broadcasted_iota(jnp.int32, (count, experts), 1).astype(jnp.float32)
    row = lax.broadcasted_iota(jnp.int32, (count, count), 0)
    col = lax.broadcasted_iota(jnp.int32, (count, count), 1)
    below = (col < row).astype(jnp.bfloat16)
    eye = (col == row).astype(jnp.bfloat16)
    each = (
        lax.broadcasted_iota(jnp.int32, (top, top * experts), 1) // experts
        == lax.broadcasted_iota(jnp.int32, (top, top * experts), 0)
    ).astype(jnp.bfloat16)
    spread = (
        lax.broadcasted_iota(jnp.int32, (experts, wide), 1) // CHUNK
        == lax.broadcasted_iota(jnp.int32, (experts, wide), 0)
    ).astype(jnp.bfloat16)
    for copy in copies[:4]:
        copy.wait()
    ids = contract(ids_ref[...].astype(jnp.bfloat16), each, ((0,), (0,)))
    gates = contract(gates_ref[...], each, ((0,), (0,)))
    picked = jnp.zeros((count, experts), jnp.float32)
    place = jnp.zeros((count, experts), jnp.float32)
    gate = jnp.zeros((count, experts), jnp.float32)
    for k in range(top):
        at = slice(k * experts, (k + 1) * experts)
        hit = ids[:, at] == lane
        picked = jnp.where(hit, 1.0, picked)
        place = jnp.where(hit, float(k), place)
        gate = jnp.where(hit, gates[:, at], gate)
    rank = contract(below, picked.astype(jnp.bfloat16), ((1,), (0,)))
    admitted = jnp.where(rank < caps_ref[...].astype(jnp.float32), picked, 0.0)
    moves = hot_ref[...].astype(jnp.float32) * odd_ref[0].astype(jnp.float32)
    moved = admitted * moves
    stay = admitted - moved
    moved_next = pltpu.roll(moved, 1, 1)
    stay_next = pltpu.roll(stay, experts - 1, 1)
    before = contract(below, (stay + moved_next).astype(jnp.bfloat16), ((1,), (0,)))
    tie_stay = jnp.where(pltpu.roll(place, 1, 1) < place, moved_next, 0.0)
    tie_move = jnp.where(pltpu.roll(place, experts - 1, 1) < place, stay_next, 0.0)
    slot = jnp.where(moves > 0, pltpu.roll(before, experts - 1, 1) + tie_move, before + tie_stay)
    code = jnp.where((admitted > 0) & (slot < SLOTS), rank, -8.0).astype(jnp.bfloat16)
    code_ref[...] = contract(code, eye, ((0,), (0,)))
    part = lax.broadcasted_iota(jnp.int32, (count, wide), 1) % CHUNK
    code_wide = contract(code, spread, ((1,), (0,)))
    gate_wide = contract(gate.astype(jnp.bfloat16), spread, ((1,), (0,)))
    put = jnp.where(code_wide == (part - SLOTS).astype(jnp.float32), gate_wide, 0.0)
    take = jnp.concatenate([(code_wide == part.astype(jnp.float32)).astype(jnp.float32), put], axis=0)
    take = take.astype(jnp.bfloat16)
    step = 4 * LANES
    for copy in copies[4:]:
        copy.wait()
    for c in range(rows_ref.shape[1] // step):
        at = slice(c * step, (c + 1) * step)
        rows = contract(take, rows_ref[:, at], ((0,), (0,)))
        sent_ref[:, at] = rows.astype(jnp.bfloat16)
        copies.append(pltpu.make_async_copy(sent_ref.at[:, at], sent_hbm.at[:, at], sems.at[6 + c]))
        copies[-1].start()
    for copy in copies[6:]:
        copy.wait()


def write_piece(part, x_ref, s_ref, hid_ref, pre_ref, out_ref):
    parts = x_ref.shape[1] * pre_ref.shape[1] * 2 // (out_ref.shape[0] * LANES)
    wide = x_ref.shape[1] // parts
    tall = pre_ref.shape[1]
    at = pl.ds(pl.multiple_of(part * wide, LANES), wide)
    up = contract(x_ref[:, at], pre_ref[...], ((0,), (0,))).astype(jnp.bfloat16)
    for c in range(tall // LANES):
        out_ref[c * wide : (c + 1) * wide, :] = up[:, c * LANES : (c + 1) * LANES]
    down = contract(hid_ref[...], s_ref[:, at], ((1,), (0,))).astype(jnp.bfloat16)
    base = wide * tall // LANES
    for c in range(wide // LANES):
        out_ref[base + c * tall : base + (c + 1) * tall, :] = down[:, c * LANES : (c + 1) * LANES]


def expert_rows(
    me_ref, recv_ref, up_ref, down_ref, own_ref, ahead_ref, behind_ref, far_ref, dot_ref,
    x_ref, s_ref, hid_ref, pre_ref,
):
    half, width = x_ref.shape
    step = half // STEPS
    lower = lax.broadcasted_iota(jnp.int32, (step, width), 0) % CHUNK < SLOTS
    lane = lax.broadcasted_iota(jnp.int32, (step, LANES), 1)
    sub = lax.broadcasted_iota(jnp.int32, (step, LANES), 0) % CHUNK
    for r in range(STEPS):
        at = slice(r * step, (r + 1) * step)
        first = recv_ref[at, :]
        second = recv_ref[r * step + half : (r + 1) * step + half, :]
        x = jnp.where(lower, first, pltpu.roll(second, SLOTS, 0))
        s = jnp.where(lower, pltpu.roll(first, step - SLOTS, 0), second)
        x_ref[at, :] = x
        s_ref[at, :] = s
        backprop = contract(s, down_ref[...], ((1,), (1,)))
        preact = contract(x, up_ref[...], ((1,), (0,)))
        sigma = jax.nn.sigmoid(preact)
        hidden = (preact * sigma).astype(jnp.bfloat16)
        hid_ref[:, at] = hidden.T
        pre_ref[at, :] = (backprop * sigma * (1.0 + preact * (1.0 - sigma))).astype(jnp.bfloat16)
        dots = jnp.sum(hidden.astype(jnp.float32) * backprop, axis=1, keepdims=True)
        groups = step // CHUNK
        spread = jnp.where(lane == sub, dots, 0.0).reshape(groups, CHUNK, LANES)
        spread = jnp.sum(spread, axis=1)
        dot_ref[r * groups : (r + 1) * groups, :] = spread
        dot_ref[(r + STEPS) * groups : (r + STEPS + 1) * groups, :] = pltpu.roll(spread, LANES - SLOTS, 1)
    parts = width * pre_ref.shape[1] * 2 // (own_ref.shape[0] * LANES)
    for shift, out_ref in ((2, far_ref), (1, ahead_ref), (3, behind_ref), (0, own_ref)):
        write_piece(lax.rem(me_ref[0] + shift, parts), x_ref, s_ref, hid_ref, pre_ref, out_ref)


def add_pieces(own_ref, far_ref, ahead_ref, behind_ref, up_ref, down_ref):
    refs = (own_ref, far_ref, ahead_ref, behind_ref)
    wide, tall = up_ref.shape
    base = wide * tall // LANES

    def total(at):
        first, second, third, fourth = [ref[at, :].astype(jnp.float32) for ref in refs]
        return ((first + second) + (third + fourth)).astype(jnp.bfloat16)

    for c in range(tall // LANES):
        up_ref[:, c * LANES : (c + 1) * LANES] = total(slice(c * wide, (c + 1) * wide))
    for c in range(wide // LANES):
        down_ref[:, c * LANES : (c + 1) * LANES] = total(slice(base + c * tall, base + (c + 1) * tall))


def gate_back(back_ref, code_ref, ids_ref, gates_ref, out_ref):
    experts, count = code_ref.shape
    code = code_ref[...]
    value = jnp.zeros((experts, count), jnp.float32)
    for j in range(SLOTS):
        value = jnp.where(code == float(j), back_ref[:, j : j + 1], value)
    row = lax.broadcasted_iota(jnp.int32, (experts, count), 0)
    for k in range(ids_ref.shape[0]):
        hit = row == ids_ref[k : k + 1, :]
        total = jnp.sum(jnp.where(hit, value, 0.0), axis=0, keepdims=True)
        out_ref[k : k + 1, :] = total / gates_ref[k : k + 1, :].astype(jnp.float32)


VMEM = pl.BlockSpec(memory_space=pltpu.VMEM)
SMEM = pl.BlockSpec(memory_space=pltpu.SMEM)
ANY = pl.BlockSpec(memory_space=pl.ANY)


def shards(tokens, cotangent, gate_values, expert_ids, hot_plan, expert_caps, w_up, w_down):
    experts = lax.axis_size("expert")
    groups = lax.axis_size("dp")
    count, width = tokens.shape
    top = gate_values.shape[1]
    hidden_width = w_up.shape[2]
    total = experts * CHUNK
    half = total // 2
    ids_t = expert_ids.T
    gates_t = gate_values.T
    me = lax.axis_index("dp").astype(jnp.int32).reshape(1)
    odd = (lax.axis_index("expert") % 2).astype(jnp.int32).reshape(1)
    whole = pltpu.CompilerParams(vmem_limit_bytes=56 << 20)
    part = pltpu.CompilerParams(vmem_limit_bytes=24 << 20)
    sent, code = pl.pallas_call(
        route_pack,
        out_shape=(
            jax.ShapeDtypeStruct((total, width), jnp.bfloat16),
            jax.ShapeDtypeStruct((experts, count), jnp.float32),
        ),
        in_specs=[SMEM, SMEM] + [ANY] * 6,
        out_specs=(ANY, VMEM),
        scratch_shapes=[
            pltpu.VMEM((top, count), jnp.int32),
            pltpu.VMEM((top, count), jnp.bfloat16),
            pltpu.VMEM((1, experts), jnp.int32),
            pltpu.VMEM((1, experts), jnp.int32),
            pltpu.VMEM((2 * count, width), jnp.bfloat16),
            pltpu.VMEM((total, width), jnp.bfloat16),
            pltpu.SemaphoreType.DMA((6 + width // 512,)),
        ],
        compiler_params=whole,
    )(me, odd, ids_t, gates_t, hot_plan.reshape(1, -1), expert_caps.reshape(1, -1), tokens, cotangent)
    recv = lax.all_to_all(
        sent.reshape(experts, CHUNK, width), "expert", split_axis=0, concat_axis=0, tiled=True
    )
    wide = width // groups
    piece = jax.ShapeDtypeStruct((2 * wide * hidden_width // LANES, LANES), jnp.bfloat16)
    own, ahead, behind, far, dots = pl.pallas_call(
        expert_rows,
        out_shape=(piece,) * 4 + (jax.ShapeDtypeStruct((experts, LANES), jnp.float32),),
        in_specs=[SMEM] + [VMEM] * 3,
        out_specs=(VMEM,) * 5,
        scratch_shapes=[
            pltpu.VMEM((half, width), jnp.bfloat16),
            pltpu.VMEM((half, width), jnp.bfloat16),
            pltpu.VMEM((hidden_width, half), jnp.bfloat16),
            pltpu.VMEM((half, hidden_width), jnp.bfloat16),
        ],
        compiler_params=part,
    )(me, recv.reshape(total, width), w_up[0], w_down[0])

    def shift(block, distance):
        return lax.ppermute(block, "dp", [(i, (i + distance) % groups) for i in range(groups)])

    far, ahead, behind = shift(far, 2), shift(ahead, 1), shift(behind, 3)
    summed_up, summed_down = pl.pallas_call(
        add_pieces,
        out_shape=(
            jax.ShapeDtypeStruct((wide, hidden_width), jnp.bfloat16),
            jax.ShapeDtypeStruct((hidden_width, wide), jnp.bfloat16),
        ),
        in_specs=[VMEM] * 4,
        out_specs=(VMEM,) * 2,
        compiler_params=pltpu.CompilerParams(vmem_limit_bytes=12 << 20),
    )(own, far, ahead, behind)
    back = lax.all_to_all(
        dots.reshape(experts, 1, LANES), "expert", split_axis=0, concat_axis=0, tiled=True
    )
    gate_grad = pl.pallas_call(
        gate_back,
        out_shape=jax.ShapeDtypeStruct((top, count), jnp.float32),
        compiler_params=pltpu.CompilerParams(vmem_limit_bytes=8 << 20),
        in_specs=[VMEM] * 4,
        out_specs=VMEM,
    )(back.reshape(experts, LANES), code, ids_t, gates_t)
    return summed_up[None], summed_down[None], gate_grad.T


def solution(mesh):
    rows = P(("dp", "expert"), None)
    return jax.shard_map(
        shards,
        mesh=mesh,
        in_specs=(rows, rows, rows, rows, P(), P(), P("expert", None, None), P("expert", None, None)),
        out_specs=(P("expert", "dp", None), P("expert", None, "dp"), rows),
        check_vma=False,
    )
```

```python
import jax
import jax.numpy as jnp
from jax import lax
from jax.experimental import pallas as pl
from jax.experimental.pallas import tpu as pltpu
from jax.sharding import PartitionSpec as P

SLOTS = 4
CHUNK = 2 * SLOTS
LANES = 128
STEPS = 1


def contract(a, b, dims):
    return lax.dot_general(a, b, (dims, ((), ())), preferred_element_type=jnp.float32)


def route_pack(
    me_ref, odd_ref, ids_hbm, gates_hbm, hot_hbm, caps_hbm, x_hbm, dy_hbm, sent_hbm, code_ref,
    ids_ref, gates_ref, hot_ref, caps_ref, rows_ref, sent_ref, sems,
):
    top, count = ids_ref.shape
    pairs = (
        (ids_hbm, ids_ref), (gates_hbm, gates_ref), (hot_hbm, hot_ref), (caps_hbm, caps_ref),
        (x_hbm, rows_ref.at[pl.ds(0, count), :]), (dy_hbm, rows_ref.at[pl.ds(count, count), :]),
    )
    copies = [pltpu.make_async_copy(a, b, sems.at[i]) for i, (a, b) in enumerate(pairs)]
    for copy in copies:
        copy.start()
    experts = hot_ref.shape[1]
    wide = experts * CHUNK
    lane = lax.broadcasted_iota(jnp.int32, (count, experts), 1).astype(jnp.float32)
    row = lax.broadcasted_iota(jnp.int32, (count, count), 0)
    col = lax.broadcasted_iota(jnp.int32, (count, count), 1)
    below = (col < row).astype(jnp.bfloat16)
    eye = (col == row).astype(jnp.bfloat16)
    each = (
        lax.broadcasted_iota(jnp.int32, (top, top * experts), 1) // experts
        == lax.broadcasted_iota(jnp.int32, (top, top * experts), 0)
    ).astype(jnp.bfloat16)
    spread = (
        lax.broadcasted_iota(jnp.int32, (experts, wide), 1) // CHUNK
        == lax.broadcasted_iota(jnp.int32, (experts, wide), 0)
    ).astype(jnp.bfloat16)
    for copy in copies[:4]:
        copy.wait()
    ids = contract(ids_ref[...].astype(jnp.bfloat16), each, ((0,), (0,)))
    gates = contract(gates_ref[...], each, ((0,), (0,)))
    picked = jnp.zeros((count, experts), jnp.float32)
    place = jnp.zeros((count, experts), jnp.float32)
    gate = jnp.zeros((count, experts), jnp.float32)
    for k in range(top):
        at = slice(k * experts, (k + 1) * experts)
        hit = ids[:, at] == lane
        picked = jnp.where(hit, 1.0, picked)
        place = jnp.where(hit, float(k), place)
        gate = jnp.where(hit, gates[:, at], gate)
    rank = contract(below, picked.astype(jnp.bfloat16), ((1,), (0,)))
    admitted = jnp.where(rank < caps_ref[...].astype(jnp.float32), picked, 0.0)
    moves = hot_ref[...].astype(jnp.float32) * odd_ref[0].astype(jnp.float32)
    moved = admitted * moves
    stay = admitted - moved
    moved_next = pltpu.roll(moved, 1, 1)
    stay_next = pltpu.roll(stay, experts - 1, 1)
    before = contract(below, (stay + moved_next).astype(jnp.bfloat16), ((1,), (0,)))
    tie_stay = jnp.where(pltpu.roll(place, 1, 1) < place, moved_next, 0.0)
    tie_move = jnp.where(pltpu.roll(place, experts - 1, 1) < place, stay_next, 0.0)
    slot = jnp.where(moves > 0, pltpu.roll(before, experts - 1, 1) + tie_move, before + tie_stay)
    code = jnp.where((admitted > 0) & (slot < SLOTS), rank, -8.0).astype(jnp.bfloat16)
    code_ref[...] = contract(code, eye, ((0,), (0,)))
    part = lax.broadcasted_iota(jnp.int32, (count, wide), 1) % CHUNK
    code_wide = contract(code, spread, ((1,), (0,)))
    gate_wide = contract(gate.astype(jnp.bfloat16), spread, ((1,), (0,)))
    put = jnp.where(code_wide == (part - SLOTS).astype(jnp.float32), gate_wide, 0.0)
    take = jnp.concatenate([(code_wide == part.astype(jnp.float32)).astype(jnp.float32), put], axis=0)
    take = take.astype(jnp.bfloat16)
    step = 4 * LANES
    for copy in copies[4:]:
        copy.wait()
    for c in range(rows_ref.shape[1] // step):
        at = slice(c * step, (c + 1) * step)
        rows = contract(take, rows_ref[:, at], ((0,), (0,)))
        sent_ref[:, at] = rows.astype(jnp.bfloat16)
        copies.append(pltpu.make_async_copy(sent_ref.at[:, at], sent_hbm.at[:, at], sems.at[6 + c]))
        copies[-1].start()
    for copy in copies[6:]:
        copy.wait()


def write_piece(part, x_ref, s_ref, hid_ref, pre_ref, out_ref):
    parts = x_ref.shape[1] * pre_ref.shape[1] * 2 // (out_ref.shape[0] * LANES)
    wide = x_ref.shape[1] // parts
    tall = pre_ref.shape[1]
    at = pl.ds(pl.multiple_of(part * wide, LANES), wide)
    up = contract(x_ref[:, at], pre_ref[...], ((0,), (0,))).astype(jnp.bfloat16)
    for c in range(tall // LANES):
        out_ref[c * wide : (c + 1) * wide, :] = up[:, c * LANES : (c + 1) * LANES]
    down = contract(hid_ref[...], s_ref[:, at], ((1,), (0,))).astype(jnp.bfloat16)
    base = wide * tall // LANES
    for c in range(wide // LANES):
        out_ref[base + c * tall : base + (c + 1) * tall, :] = down[:, c * LANES : (c + 1) * LANES]


def expert_rows(
    me_ref, recv_ref, up_ref, down_ref, own_ref, ahead_ref, behind_ref, far_ref, dot_ref,
    x_ref, s_ref, hid_ref, pre_ref,
):
    half, width = x_ref.shape
    step = half // STEPS
    lower = lax.broadcasted_iota(jnp.int32, (step, width), 0) % CHUNK < SLOTS
    lane = lax.broadcasted_iota(jnp.int32, (step, LANES), 1)
    sub = lax.broadcasted_iota(jnp.int32, (step, LANES), 0) % CHUNK
    for r in range(STEPS):
        at = slice(r * step, (r + 1) * step)
        first = recv_ref[at, :]
        second = recv_ref[r * step + half : (r + 1) * step + half, :]
        x = jnp.where(lower, first, pltpu.roll(second, SLOTS, 0))
        s = jnp.where(lower, pltpu.roll(first, step - SLOTS, 0), second)
        x_ref[at, :] = x
        s_ref[at, :] = s
        backprop = contract(s, down_ref[...], ((1,), (1,)))
        preact = contract(x, up_ref[...], ((1,), (0,)))
        sigma = jax.nn.sigmoid(preact)
        hidden = (preact * sigma).astype(jnp.bfloat16)
        hid_ref[:, at] = hidden.T
        pre_ref[at, :] = (backprop * sigma * (1.0 + preact * (1.0 - sigma))).astype(jnp.bfloat16)
        dots = jnp.sum(hidden.astype(jnp.float32) * backprop, axis=1, keepdims=True)
        groups = step // CHUNK
        spread = jnp.where(lane == sub, dots, 0.0).reshape(groups, CHUNK, LANES)
        spread = jnp.sum(spread, axis=1)
        dot_ref[r * groups : (r + 1) * groups, :] = spread
        dot_ref[(r + STEPS) * groups : (r + STEPS + 1) * groups, :] = pltpu.roll(spread, LANES - SLOTS, 1)
    parts = width * pre_ref.shape[1] * 2 // (own_ref.shape[0] * LANES)
    for shift, out_ref in ((1, ahead_ref), (3, behind_ref), (2, far_ref), (0, own_ref)):
        write_piece(lax.rem(me_ref[0] + shift, parts), x_ref, s_ref, hid_ref, pre_ref, out_ref)


def add_pieces(own_ref, ahead_ref, behind_ref, far_ref, up_ref, down_ref):
    refs = (own_ref, far_ref, ahead_ref, behind_ref)
    wide, tall = up_ref.shape
    base = wide * tall // LANES

    def total(at):
        first, second, third, fourth = [ref[at, :].astype(jnp.float32) for ref in refs]
        return ((first + second) + (third + fourth)).astype(jnp.bfloat16)

    for c in range(tall // LANES):
        up_ref[:, c * LANES : (c + 1) * LANES] = total(slice(c * wide, (c + 1) * wide))
    for c in range(wide // LANES):
        down_ref[:, c * LANES : (c + 1) * LANES] = total(slice(base + c * tall, base + (c + 1) * tall))


def gate_back(back_ref, code_ref, ids_ref, gates_ref, out_ref):
    experts, count = code_ref.shape
    code = code_ref[...]
    value = jnp.zeros((experts, count), jnp.float32)
    for j in range(SLOTS):
        value = jnp.where(code == float(j), back_ref[:, j : j + 1], value)
    row = lax.broadcasted_iota(jnp.int32, (experts, count), 0)
    for k in range(ids_ref.shape[0]):
        hit = row == ids_ref[k : k + 1, :]
        total = jnp.sum(jnp.where(hit, value, 0.0), axis=0, keepdims=True)
        out_ref[k : k + 1, :] = total / gates_ref[k : k + 1, :].astype(jnp.float32)


VMEM = pl.BlockSpec(memory_space=pltpu.VMEM)
SMEM = pl.BlockSpec(memory_space=pltpu.SMEM)
ANY = pl.BlockSpec(memory_space=pl.ANY)


def shards(tokens, cotangent, gate_values, expert_ids, hot_plan, expert_caps, w_up, w_down):
    experts = lax.axis_size("expert")
    groups = lax.axis_size("dp")
    count, width = tokens.shape
    top = gate_values.shape[1]
    hidden_width = w_up.shape[2]
    total = experts * CHUNK
    half = total // 2
    ids_t = expert_ids.T
    gates_t = gate_values.T
    me = lax.axis_index("dp").astype(jnp.int32).reshape(1)
    odd = (lax.axis_index("expert") % 2).astype(jnp.int32).reshape(1)
    whole = pltpu.CompilerParams(vmem_limit_bytes=56 << 20)
    part = pltpu.CompilerParams(vmem_limit_bytes=24 << 20)
    sent, code = pl.pallas_call(
        route_pack,
        out_shape=(
            jax.ShapeDtypeStruct((total, width), jnp.bfloat16),
            jax.ShapeDtypeStruct((experts, count), jnp.float32),
        ),
        in_specs=[SMEM, SMEM] + [ANY] * 6,
        out_specs=(ANY, VMEM),
        scratch_shapes=[
            pltpu.VMEM((top, count), jnp.int32),
            pltpu.VMEM((top, count), jnp.bfloat16),
            pltpu.VMEM((1, experts), jnp.int32),
            pltpu.VMEM((1, experts), jnp.int32),
            pltpu.VMEM((2 * count, width), jnp.bfloat16),
            pltpu.VMEM((total, width), jnp.bfloat16),
            pltpu.SemaphoreType.DMA((6 + width // 512,)),
        ],
        compiler_params=whole,
    )(me, odd, ids_t, gates_t, hot_plan.reshape(1, -1), expert_caps.reshape(1, -1), tokens, cotangent)
    recv = lax.all_to_all(
        sent.reshape(experts, CHUNK, width), "expert", split_axis=0, concat_axis=0, tiled=True
    )
    wide = width // groups
    piece = jax.ShapeDtypeStruct((2 * wide * hidden_width // LANES, LANES), jnp.bfloat16)
    own, ahead, behind, far, dots = pl.pallas_call(
        expert_rows,
        out_shape=(piece,) * 4 + (jax.ShapeDtypeStruct((experts, LANES), jnp.float32),),
        in_specs=[SMEM] + [VMEM] * 3,
        out_specs=(VMEM,) * 5,
        scratch_shapes=[
            pltpu.VMEM((half, width), jnp.bfloat16),
            pltpu.VMEM((half, width), jnp.bfloat16),
            pltpu.VMEM((hidden_width, half), jnp.bfloat16),
            pltpu.VMEM((half, hidden_width), jnp.bfloat16),
        ],
        compiler_params=part,
    )(me, recv.reshape(total, width), w_up[0], w_down[0])

    def shift(block, distance):
        return lax.ppermute(block, "dp", [(i, (i + distance) % groups) for i in range(groups)])

    ahead, behind, far = shift(ahead, 1), shift(behind, 3), shift(far, 2)
    summed_up, summed_down = pl.pallas_call(
        add_pieces,
        out_shape=(
            jax.ShapeDtypeStruct((wide, hidden_width), jnp.bfloat16),
            jax.ShapeDtypeStruct((hidden_width, wide), jnp.bfloat16),
        ),
        in_specs=[VMEM] * 4,
        out_specs=(VMEM,) * 2,
        compiler_params=pltpu.CompilerParams(vmem_limit_bytes=12 << 20),
    )(own, ahead, behind, far)
    back = lax.all_to_all(
        dots.reshape(experts, 1, LANES), "expert", split_axis=0, concat_axis=0, tiled=True
    )
    gate_grad = pl.pallas_call(
        gate_back,
        out_shape=jax.ShapeDtypeStruct((top, count), jnp.float32),
        compiler_params=pltpu.CompilerParams(vmem_limit_bytes=8 << 20),
        in_specs=[VMEM] * 4,
        out_specs=VMEM,
    )(back.reshape(experts, LANES), code, ids_t, gates_t)
    return summed_up[None], summed_down[None], gate_grad.T


def solution(mesh):
    rows = P(("dp", "expert"), None)
    return jax.shard_map(
        shards,
        mesh=mesh,
        in_specs=(rows, rows, rows, rows, P(), P(), P("expert", None, None), P("expert", None, None)),
        out_specs=(P("expert", "dp", None), P("expert", None, "dp"), rows),
        check_vma=False,
    )
```

```python
import jax
import jax.numpy as jnp
from jax import lax
from jax.experimental import pallas as pl
from jax.experimental.pallas import tpu as pltpu
from jax.sharding import PartitionSpec as P

SLOTS = 4
CHUNK = 2 * SLOTS
LANES = 128
STEPS = 1


def contract(a, b, dims):
    return lax.dot_general(a, b, (dims, ((), ())), preferred_element_type=jnp.float32)


def route_pack(
    me_ref, odd_ref, ids_hbm, gates_hbm, hot_hbm, caps_hbm, x_hbm, dy_hbm, sent_hbm, code_ref,
    ids_ref, gates_ref, hot_ref, caps_ref, rows_ref, sent_ref, sems,
):
    top, count = ids_ref.shape
    pairs = (
        (ids_hbm, ids_ref), (gates_hbm, gates_ref), (hot_hbm, hot_ref), (caps_hbm, caps_ref),
        (x_hbm, rows_ref.at[pl.ds(0, count), :]), (dy_hbm, rows_ref.at[pl.ds(count, count), :]),
    )
    copies = [pltpu.make_async_copy(a, b, sems.at[i]) for i, (a, b) in enumerate(pairs)]
    for copy in copies:
        copy.start()
    experts = hot_ref.shape[1]
    wide = experts * CHUNK
    lane = lax.broadcasted_iota(jnp.int32, (count, experts), 1).astype(jnp.float32)
    row = lax.broadcasted_iota(jnp.int32, (count, count), 0)
    col = lax.broadcasted_iota(jnp.int32, (count, count), 1)
    below = (col < row).astype(jnp.bfloat16)
    eye = (col == row).astype(jnp.bfloat16)
    each = (
        lax.broadcasted_iota(jnp.int32, (top, top * experts), 1) // experts
        == lax.broadcasted_iota(jnp.int32, (top, top * experts), 0)
    ).astype(jnp.bfloat16)
    spread = (
        lax.broadcasted_iota(jnp.int32, (experts, wide), 1) // CHUNK
        == lax.broadcasted_iota(jnp.int32, (experts, wide), 0)
    ).astype(jnp.bfloat16)
    for copy in copies[:4]:
        copy.wait()
    ids = contract(ids_ref[...].astype(jnp.bfloat16), each, ((0,), (0,)))
    gates = contract(gates_ref[...], each, ((0,), (0,)))
    picked = jnp.zeros((count, experts), jnp.float32)
    place = jnp.zeros((count, experts), jnp.float32)
    gate = jnp.zeros((count, experts), jnp.float32)
    for k in range(top):
        at = slice(k * experts, (k + 1) * experts)
        hit = ids[:, at] == lane
        picked = jnp.where(hit, 1.0, picked)
        place = jnp.where(hit, float(k), place)
        gate = jnp.where(hit, gates[:, at], gate)
    rank = contract(below, picked.astype(jnp.bfloat16), ((1,), (0,)))
    admitted = jnp.where(rank < caps_ref[...].astype(jnp.float32), picked, 0.0)
    moves = hot_ref[...].astype(jnp.float32) * odd_ref[0].astype(jnp.float32)
    moved = admitted * moves
    stay = admitted - moved
    moved_next = pltpu.roll(moved, 1, 1)
    stay_next = pltpu.roll(stay, experts - 1, 1)
    before = contract(below, (stay + moved_next).astype(jnp.bfloat16), ((1,), (0,)))
    tie_stay = jnp.where(pltpu.roll(place, 1, 1) < place, moved_next, 0.0)
    tie_move = jnp.where(pltpu.roll(place, experts - 1, 1) < place, stay_next, 0.0)
    slot = jnp.where(moves > 0, pltpu.roll(before, experts - 1, 1) + tie_move, before + tie_stay)
    code = jnp.where((admitted > 0) & (slot < SLOTS), rank, -8.0).astype(jnp.bfloat16)
    code_ref[...] = contract(code, eye, ((0,), (0,)))
    part = lax.broadcasted_iota(jnp.int32, (count, wide), 1) % CHUNK
    code_wide = contract(code, spread, ((1,), (0,)))
    gate_wide = contract(gate.astype(jnp.bfloat16), spread, ((1,), (0,)))
    put = jnp.where(code_wide == (part - SLOTS).astype(jnp.float32), gate_wide, 0.0)
    take = jnp.concatenate([(code_wide == part.astype(jnp.float32)).astype(jnp.float32), put], axis=0)
    take = take.astype(jnp.bfloat16)
    step = 4 * LANES
    for copy in copies[4:]:
        copy.wait()
    for c in range(rows_ref.shape[1] // step):
        at = slice(c * step, (c + 1) * step)
        rows = contract(take, rows_ref[:, at], ((0,), (0,)))
        sent_ref[:, at] = rows.astype(jnp.bfloat16)
        copies.append(pltpu.make_async_copy(sent_ref.at[:, at], sent_hbm.at[:, at], sems.at[6 + c]))
        copies[-1].start()
    for copy in copies[6:]:
        copy.wait()


def write_piece(part, x_ref, s_ref, hid_ref, pre_ref, out_ref):
    parts = x_ref.shape[1] * pre_ref.shape[1] * 2 // (out_ref.shape[0] * LANES)
    wide = x_ref.shape[1] // parts
    tall = pre_ref.shape[1]
    at = pl.ds(pl.multiple_of(part * wide, LANES), wide)
    up = contract(x_ref[:, at], pre_ref[...], ((0,), (0,))).astype(jnp.bfloat16)
    for c in range(tall // LANES):
        out_ref[c * wide : (c + 1) * wide, :] = up[:, c * LANES : (c + 1) * LANES]
    down = contract(hid_ref[...], s_ref[:, at], ((1,), (0,))).astype(jnp.bfloat16)
    base = wide * tall // LANES
    for c in range(wide // LANES):
        out_ref[base + c * tall : base + (c + 1) * tall, :] = down[:, c * LANES : (c + 1) * LANES]


def expert_rows(
    me_ref, recv_ref, up_ref, down_ref, own_ref, ahead_ref, behind_ref, far_ref, dot_ref,
    x_ref, s_ref, hid_ref, pre_ref,
):
    half, width = x_ref.shape
    step = half // STEPS
    lower = lax.broadcasted_iota(jnp.int32, (step, width), 0) % CHUNK < SLOTS
    lane = lax.broadcasted_iota(jnp.int32, (step, LANES), 1)
    sub = lax.broadcasted_iota(jnp.int32, (step, LANES), 0) % CHUNK
    for r in range(STEPS):
        at = slice(r * step, (r + 1) * step)
        first = recv_ref[at, :]
        second = recv_ref[r * step + half : (r + 1) * step + half, :]
        x = jnp.where(lower, first, pltpu.roll(second, SLOTS, 0))
        s = jnp.where(lower, pltpu.roll(first, step - SLOTS, 0), second)
        x_ref[at, :] = x
        s_ref[at, :] = s
        backprop = contract(s, down_ref[...], ((1,), (1,)))
        preact = contract(x, up_ref[...], ((1,), (0,)))
        sigma = jax.nn.sigmoid(preact)
        hidden = (preact * sigma).astype(jnp.bfloat16)
        hid_ref[:, at] = hidden.T
        pre_ref[at, :] = (backprop * sigma * (1.0 + preact * (1.0 - sigma))).astype(jnp.bfloat16)
        dots = jnp.sum(hidden.astype(jnp.float32) * backprop, axis=1, keepdims=True)
        groups = step // CHUNK
        spread = jnp.where(lane == sub, dots, 0.0).reshape(groups, CHUNK, LANES)
        spread = jnp.sum(spread, axis=1)
        dot_ref[r * groups : (r + 1) * groups, :] = spread
        dot_ref[(r + STEPS) * groups : (r + STEPS + 1) * groups, :] = pltpu.roll(spread, LANES - SLOTS, 1)
    parts = width * pre_ref.shape[1] * 2 // (own_ref.shape[0] * LANES)
    for shift, out_ref in ((1, ahead_ref), (2, far_ref), (3, behind_ref), (0, own_ref)):
        write_piece(lax.rem(me_ref[0] + shift, parts), x_ref, s_ref, hid_ref, pre_ref, out_ref)


def add_pieces(own_ref, ahead_ref, far_ref, behind_ref, up_ref, down_ref):
    refs = (own_ref, far_ref, ahead_ref, behind_ref)
    wide, tall = up_ref.shape
    base = wide * tall // LANES

    def total(at):
        first, second, third, fourth = [ref[at, :].astype(jnp.float32) for ref in refs]
        return ((first + second) + (third + fourth)).astype(jnp.bfloat16)

    for c in range(tall // LANES):
        up_ref[:, c * LANES : (c + 1) * LANES] = total(slice(c * wide, (c + 1) * wide))
    for c in range(wide // LANES):
        down_ref[:, c * LANES : (c + 1) * LANES] = total(slice(base + c * tall, base + (c + 1) * tall))


def gate_back(back_ref, code_ref, ids_ref, gates_ref, out_ref):
    experts, count = code_ref.shape
    code = code_ref[...]
    value = jnp.zeros((experts, count), jnp.float32)
    for j in range(SLOTS):
        value = jnp.where(code == float(j), back_ref[:, j : j + 1], value)
    row = lax.broadcasted_iota(jnp.int32, (experts, count), 0)
    for k in range(ids_ref.shape[0]):
        hit = row == ids_ref[k : k + 1, :]
        total = jnp.sum(jnp.where(hit, value, 0.0), axis=0, keepdims=True)
        out_ref[k : k + 1, :] = total / gates_ref[k : k + 1, :].astype(jnp.float32)


VMEM = pl.BlockSpec(memory_space=pltpu.VMEM)
SMEM = pl.BlockSpec(memory_space=pltpu.SMEM)
ANY = pl.BlockSpec(memory_space=pl.ANY)


def shards(tokens, cotangent, gate_values, expert_ids, hot_plan, expert_caps, w_up, w_down):
    experts = lax.axis_size("expert")
    groups = lax.axis_size("dp")
    count, width = tokens.shape
    top = gate_values.shape[1]
    hidden_width = w_up.shape[2]
    total = experts * CHUNK
    half = total // 2
    ids_t = expert_ids.T
    gates_t = gate_values.T
    me = lax.axis_index("dp").astype(jnp.int32).reshape(1)
    odd = (lax.axis_index("expert") % 2).astype(jnp.int32).reshape(1)
    whole = pltpu.CompilerParams(vmem_limit_bytes=56 << 20)
    part = pltpu.CompilerParams(vmem_limit_bytes=24 << 20)
    sent, code = pl.pallas_call(
        route_pack,
        out_shape=(
            jax.ShapeDtypeStruct((total, width), jnp.bfloat16),
            jax.ShapeDtypeStruct((experts, count), jnp.float32),
        ),
        in_specs=[SMEM, SMEM] + [ANY] * 6,
        out_specs=(ANY, VMEM),
        scratch_shapes=[
            pltpu.VMEM((top, count), jnp.int32),
            pltpu.VMEM((top, count), jnp.bfloat16),
            pltpu.VMEM((1, experts), jnp.int32),
            pltpu.VMEM((1, experts), jnp.int32),
            pltpu.VMEM((2 * count, width), jnp.bfloat16),
            pltpu.VMEM((total, width), jnp.bfloat16),
            pltpu.SemaphoreType.DMA((6 + width // 512,)),
        ],
        compiler_params=whole,
    )(me, odd, ids_t, gates_t, hot_plan.reshape(1, -1), expert_caps.reshape(1, -1), tokens, cotangent)
    recv = lax.all_to_all(
        sent.reshape(experts, CHUNK, width), "expert", split_axis=0, concat_axis=0, tiled=True
    )
    wide = width // groups
    piece = jax.ShapeDtypeStruct((2 * wide * hidden_width // LANES, LANES), jnp.bfloat16)
    own, ahead, behind, far, dots = pl.pallas_call(
        expert_rows,
        out_shape=(piece,) * 4 + (jax.ShapeDtypeStruct((experts, LANES), jnp.float32),),
        in_specs=[SMEM] + [VMEM] * 3,
        out_specs=(VMEM,) * 5,
        scratch_shapes=[
            pltpu.VMEM((half, width), jnp.bfloat16),
            pltpu.VMEM((half, width), jnp.bfloat16),
            pltpu.VMEM((hidden_width, half), jnp.bfloat16),
            pltpu.VMEM((half, hidden_width), jnp.bfloat16),
        ],
        compiler_params=part,
    )(me, recv.reshape(total, width), w_up[0], w_down[0])

    def shift(block, distance):
        return lax.ppermute(block, "dp", [(i, (i + distance) % groups) for i in range(groups)])

    ahead, far, behind = shift(ahead, 1), shift(far, 2), shift(behind, 3)
    summed_up, summed_down = pl.pallas_call(
        add_pieces,
        out_shape=(
            jax.ShapeDtypeStruct((wide, hidden_width), jnp.bfloat16),
            jax.ShapeDtypeStruct((hidden_width, wide), jnp.bfloat16),
        ),
        in_specs=[VMEM] * 4,
        out_specs=(VMEM,) * 2,
        compiler_params=pltpu.CompilerParams(vmem_limit_bytes=12 << 20),
    )(own, ahead, far, behind)
    back = lax.all_to_all(
        dots.reshape(experts, 1, LANES), "expert", split_axis=0, concat_axis=0, tiled=True
    )
    gate_grad = pl.pallas_call(
        gate_back,
        out_shape=jax.ShapeDtypeStruct((top, count), jnp.float32),
        compiler_params=pltpu.CompilerParams(vmem_limit_bytes=8 << 20),
        in_specs=[VMEM] * 4,
        out_specs=VMEM,
    )(back.reshape(experts, LANES), code, ids_t, gates_t)
    return summed_up[None], summed_down[None], gate_grad.T


def solution(mesh):
    rows = P(("dp", "expert"), None)
    return jax.shard_map(
        shards,
        mesh=mesh,
        in_specs=(rows, rows, rows, rows, P(), P(), P("expert", None, None), P("expert", None, None)),
        out_specs=(P("expert", "dp", None), P("expert", None, "dp"), rows),
        check_vma=False,
    )
```

```python
import jax
import jax.numpy as jnp
from jax import lax
from jax.experimental import pallas as pl
from jax.experimental.pallas import tpu as pltpu
from jax.sharding import PartitionSpec as P

SLOTS = 4
CHUNK = 2 * SLOTS
LANES = 128
STEPS = 1


def contract(a, b, dims):
    return lax.dot_general(a, b, (dims, ((), ())), preferred_element_type=jnp.float32)


def route_pack(
    me_ref, odd_ref, ids_hbm, gates_hbm, hot_hbm, caps_hbm, x_hbm, dy_hbm, sent_hbm, code_ref,
    ids_ref, gates_ref, hot_ref, caps_ref, rows_ref, sent_ref, sems,
):
    top, count = ids_ref.shape
    pairs = (
        (ids_hbm, ids_ref), (gates_hbm, gates_ref), (hot_hbm, hot_ref), (caps_hbm, caps_ref),
        (x_hbm, rows_ref.at[pl.ds(0, count), :]), (dy_hbm, rows_ref.at[pl.ds(count, count), :]),
    )
    copies = [pltpu.make_async_copy(a, b, sems.at[i]) for i, (a, b) in enumerate(pairs)]
    for copy in copies:
        copy.start()
    experts = hot_ref.shape[1]
    wide = experts * CHUNK
    lane = lax.broadcasted_iota(jnp.int32, (count, experts), 1).astype(jnp.float32)
    row = lax.broadcasted_iota(jnp.int32, (count, count), 0)
    col = lax.broadcasted_iota(jnp.int32, (count, count), 1)
    below = (col < row).astype(jnp.bfloat16)
    eye = (col == row).astype(jnp.bfloat16)
    each = (
        lax.broadcasted_iota(jnp.int32, (top, top * experts), 1) // experts
        == lax.broadcasted_iota(jnp.int32, (top, top * experts), 0)
    ).astype(jnp.bfloat16)
    spread = (
        lax.broadcasted_iota(jnp.int32, (experts, wide), 1) // CHUNK
        == lax.broadcasted_iota(jnp.int32, (experts, wide), 0)
    ).astype(jnp.bfloat16)
    for copy in copies[:4]:
        copy.wait()
    ids = contract(ids_ref[...].astype(jnp.bfloat16), each, ((0,), (0,)))
    gates = contract(gates_ref[...], each, ((0,), (0,)))
    picked = jnp.zeros((count, experts), jnp.float32)
    place = jnp.zeros((count, experts), jnp.float32)
    gate = jnp.zeros((count, experts), jnp.float32)
    for k in range(top):
        at = slice(k * experts, (k + 1) * experts)
        hit = ids[:, at] == lane
        picked = jnp.where(hit, 1.0, picked)
        place = jnp.where(hit, float(k), place)
        gate = jnp.where(hit, gates[:, at], gate)
    rank = contract(below, picked.astype(jnp.bfloat16), ((1,), (0,)))
    admitted = jnp.where(rank < caps_ref[...].astype(jnp.float32), picked, 0.0)
    moves = hot_ref[...].astype(jnp.float32) * odd_ref[0].astype(jnp.float32)
    moved = admitted * moves
    stay = admitted - moved
    moved_next = pltpu.roll(moved, 1, 1)
    stay_next = pltpu.roll(stay, experts - 1, 1)
    before = contract(below, (stay + moved_next).astype(jnp.bfloat16), ((1,), (0,)))
    tie_stay = jnp.where(pltpu.roll(place, 1, 1) < place, moved_next, 0.0)
    tie_move = jnp.where(pltpu.roll(place, experts - 1, 1) < place, stay_next, 0.0)
    slot = jnp.where(moves > 0, pltpu.roll(before, experts - 1, 1) + tie_move, before + tie_stay)
    code = jnp.where((admitted > 0) & (slot < SLOTS), rank, -8.0).astype(jnp.bfloat16)
    code_ref[...] = contract(code, eye, ((0,), (0,)))
    part = lax.broadcasted_iota(jnp.int32, (count, wide), 1) % CHUNK
    code_wide = contract(code, spread, ((1,), (0,)))
    gate_wide = contract(gate.astype(jnp.bfloat16), spread, ((1,), (0,)))
    put = jnp.where(code_wide == (part - SLOTS).astype(jnp.float32), gate_wide, 0.0)
    take = jnp.concatenate([(code_wide == part.astype(jnp.float32)).astype(jnp.float32), put], axis=0)
    take = take.astype(jnp.bfloat16)
    step = 4 * LANES
    for copy in copies[4:]:
        copy.wait()
    for c in range(rows_ref.shape[1] // step):
        at = slice(c * step, (c + 1) * step)
        rows = contract(take, rows_ref[:, at], ((0,), (0,)))
        sent_ref[:, at] = rows.astype(jnp.bfloat16)
        copies.append(pltpu.make_async_copy(sent_ref.at[:, at], sent_hbm.at[:, at], sems.at[6 + c]))
        copies[-1].start()
    for copy in copies[6:]:
        copy.wait()


def write_piece(part, x_ref, s_ref, hid_ref, pre_ref, out_ref):
    parts = x_ref.shape[1] * pre_ref.shape[1] * 2 // (out_ref.shape[0] * LANES)
    wide = x_ref.shape[1] // parts
    tall = pre_ref.shape[1]
    at = pl.ds(pl.multiple_of(part * wide, LANES), wide)
    up = contract(x_ref[:, at], pre_ref[...], ((0,), (0,))).astype(jnp.bfloat16)
    for c in range(tall // LANES):
        out_ref[c * wide : (c + 1) * wide, :] = up[:, c * LANES : (c + 1) * LANES]
    down = contract(hid_ref[...], s_ref[:, at], ((1,), (0,))).astype(jnp.bfloat16)
    base = wide * tall // LANES
    for c in range(wide // LANES):
        out_ref[base + c * tall : base + (c + 1) * tall, :] = down[:, c * LANES : (c + 1) * LANES]


def expert_rows(
    me_ref, recv_ref, up_ref, down_ref, own_ref, ahead_ref, behind_ref, far_ref, dot_ref,
    x_ref, s_ref, hid_ref, pre_ref,
):
    half, width = x_ref.shape
    step = half // STEPS
    lower = lax.broadcasted_iota(jnp.int32, (step, width), 0) % CHUNK < SLOTS
    lane = lax.broadcasted_iota(jnp.int32, (step, LANES), 1)
    sub = lax.broadcasted_iota(jnp.int32, (step, LANES), 0) % CHUNK
    for r in range(STEPS):
        at = slice(r * step, (r + 1) * step)
        first = recv_ref[at, :]
        second = recv_ref[r * step + half : (r + 1) * step + half, :]
        x = jnp.where(lower, first, pltpu.roll(second, SLOTS, 0))
        s = jnp.where(lower, pltpu.roll(first, step - SLOTS, 0), second)
        x_ref[at, :] = x
        s_ref[at, :] = s
        backprop = contract(s, down_ref[...], ((1,), (1,)))
        preact = contract(x, up_ref[...], ((1,), (0,)))
        sigma = jax.nn.sigmoid(preact)
        hidden = (preact * sigma).astype(jnp.bfloat16)
        hid_ref[:, at] = hidden.T
        pre_ref[at, :] = (backprop * sigma * (1.0 + preact * (1.0 - sigma))).astype(jnp.bfloat16)
        dots = jnp.sum(hidden.astype(jnp.float32) * backprop, axis=1, keepdims=True)
        groups = step // CHUNK
        spread = jnp.where(lane == sub, dots, 0.0).reshape(groups, CHUNK, LANES)
        spread = jnp.sum(spread, axis=1)
        dot_ref[r * groups : (r + 1) * groups, :] = spread
        dot_ref[(r + STEPS) * groups : (r + STEPS + 1) * groups, :] = pltpu.roll(spread, LANES - SLOTS, 1)
    parts = width * pre_ref.shape[1] * 2 // (own_ref.shape[0] * LANES)
    for shift, out_ref in ((2, far_ref), (3, behind_ref), (1, ahead_ref), (0, own_ref)):
        write_piece(lax.rem(me_ref[0] + shift, parts), x_ref, s_ref, hid_ref, pre_ref, out_ref)


def add_pieces(own_ref, far_ref, behind_ref, ahead_ref, up_ref, down_ref):
    refs = (own_ref, far_ref, ahead_ref, behind_ref)
    wide, tall = up_ref.shape
    base = wide * tall // LANES

    def total(at):
        first, second, third, fourth = [ref[at, :].astype(jnp.float32) for ref in refs]
        return ((first + second) + (third + fourth)).astype(jnp.bfloat16)

    for c in range(tall // LANES):
        up_ref[:, c * LANES : (c + 1) * LANES] = total(slice(c * wide, (c + 1) * wide))
    for c in range(wide // LANES):
        down_ref[:, c * LANES : (c + 1) * LANES] = total(slice(base + c * tall, base + (c + 1) * tall))


def gate_back(back_ref, code_ref, ids_ref, gates_ref, out_ref):
    experts, count = code_ref.shape
    code = code_ref[...]
    value = jnp.zeros((experts, count), jnp.float32)
    for j in range(SLOTS):
        value = jnp.where(code == float(j), back_ref[:, j : j + 1], value)
    row = lax.broadcasted_iota(jnp.int32, (experts, count), 0)
    for k in range(ids_ref.shape[0]):
        hit = row == ids_ref[k : k + 1, :]
        total = jnp.sum(jnp.where(hit, value, 0.0), axis=0, keepdims=True)
        out_ref[k : k + 1, :] = total / gates_ref[k : k + 1, :].astype(jnp.float32)


VMEM = pl.BlockSpec(memory_space=pltpu.VMEM)
SMEM = pl.BlockSpec(memory_space=pltpu.SMEM)
ANY = pl.BlockSpec(memory_space=pl.ANY)


def shards(tokens, cotangent, gate_values, expert_ids, hot_plan, expert_caps, w_up, w_down):
    experts = lax.axis_size("expert")
    groups = lax.axis_size("dp")
    count, width = tokens.shape
    top = gate_values.shape[1]
    hidden_width = w_up.shape[2]
    total = experts * CHUNK
    half = total // 2
    ids_t = expert_ids.T
    gates_t = gate_values.T
    me = lax.axis_index("dp").astype(jnp.int32).reshape(1)
    odd = (lax.axis_index("expert") % 2).astype(jnp.int32).reshape(1)
    whole = pltpu.CompilerParams(vmem_limit_bytes=56 << 20)
    part = pltpu.CompilerParams(vmem_limit_bytes=24 << 20)
    sent, code = pl.pallas_call(
        route_pack,
        out_shape=(
            jax.ShapeDtypeStruct((total, width), jnp.bfloat16),
            jax.ShapeDtypeStruct((experts, count), jnp.float32),
        ),
        in_specs=[SMEM, SMEM] + [ANY] * 6,
        out_specs=(ANY, VMEM),
        scratch_shapes=[
            pltpu.VMEM((top, count), jnp.int32),
            pltpu.VMEM((top, count), jnp.bfloat16),
            pltpu.VMEM((1, experts), jnp.int32),
            pltpu.VMEM((1, experts), jnp.int32),
            pltpu.VMEM((2 * count, width), jnp.bfloat16),
            pltpu.VMEM((total, width), jnp.bfloat16),
            pltpu.SemaphoreType.DMA((6 + width // 512,)),
        ],
        compiler_params=whole,
    )(me, odd, ids_t, gates_t, hot_plan.reshape(1, -1), expert_caps.reshape(1, -1), tokens, cotangent)
    recv = lax.all_to_all(
        sent.reshape(experts, CHUNK, width), "expert", split_axis=0, concat_axis=0, tiled=True
    )
    wide = width // groups
    piece = jax.ShapeDtypeStruct((2 * wide * hidden_width // LANES, LANES), jnp.bfloat16)
    own, ahead, behind, far, dots = pl.pallas_call(
        expert_rows,
        out_shape=(piece,) * 4 + (jax.ShapeDtypeStruct((experts, LANES), jnp.float32),),
        in_specs=[SMEM] + [VMEM] * 3,
        out_specs=(VMEM,) * 5,
        scratch_shapes=[
            pltpu.VMEM((half, width), jnp.bfloat16),
            pltpu.VMEM((half, width), jnp.bfloat16),
            pltpu.VMEM((hidden_width, half), jnp.bfloat16),
            pltpu.VMEM((half, hidden_width), jnp.bfloat16),
        ],
        compiler_params=part,
    )(me, recv.reshape(total, width), w_up[0], w_down[0])

    def shift(block, distance):
        return lax.ppermute(block, "dp", [(i, (i + distance) % groups) for i in range(groups)])

    far, behind, ahead = shift(far, 2), shift(behind, 3), shift(ahead, 1)
    summed_up, summed_down = pl.pallas_call(
        add_pieces,
        out_shape=(
            jax.ShapeDtypeStruct((wide, hidden_width), jnp.bfloat16),
            jax.ShapeDtypeStruct((hidden_width, wide), jnp.bfloat16),
        ),
        in_specs=[VMEM] * 4,
        out_specs=(VMEM,) * 2,
        compiler_params=pltpu.CompilerParams(vmem_limit_bytes=12 << 20),
    )(own, far, behind, ahead)
    back = lax.all_to_all(
        dots.reshape(experts, 1, LANES), "expert", split_axis=0, concat_axis=0, tiled=True
    )
    gate_grad = pl.pallas_call(
        gate_back,
        out_shape=jax.ShapeDtypeStruct((top, count), jnp.float32),
        compiler_params=pltpu.CompilerParams(vmem_limit_bytes=8 << 20),
        in_specs=[VMEM] * 4,
        out_specs=VMEM,
    )(back.reshape(experts, LANES), code, ids_t, gates_t)
    return summed_up[None], summed_down[None], gate_grad.T


def solution(mesh):
    rows = P(("dp", "expert"), None)
    return jax.shard_map(
        shards,
        mesh=mesh,
        in_specs=(rows, rows, rows, rows, P(), P(), P("expert", None, None), P("expert", None, None)),
        out_specs=(P("expert", "dp", None), P("expert", None, "dp"), rows),
        check_vma=False,
    )
```
